256 devices in a mesh: head: 4 (over x_hi, core), inner: 8 (over z), outer: 8 (over y, x_lo).
Axes of the slice: x: 4 (x_hi: 2, x_lo: 2; x = x_hi * 2 + x_lo), y: 4, z: 8, core: 2. Of those that a mesh axis runs over, the one named last changes fastest.
Arguments:
- query: bfloat16 [32768, 4096], P(('head', 'inner', 'outer')), may hold values from -4.5 to 4.5, as said below
- key_value: bfloat16 [32768, 1024], P(('head', 'inner', 'outer')), may hold values from -4.5 to 4.5
- grad_out: bfloat16 [32768, 4096], P(('head', 'inner', 'outer')), may hold values from -6 to 6
- positions: int32 [32768], P(('head', 'inner', 'outer')), may hold values from 0 to 32767, as said below
Outputs:
- attn_out: bfloat16 [32768, 4096], P(('head', 'inner', 'outer'))
- grad_query: bfloat16 [32768, 4096], P(('head', 'inner', 'outer'))
- grad_kv: float32 [32768, 1024], P(('head', 'inner', 'outer'))
The draws below stay inside these ranges and needn't reach their ends.
Inputs may be any that keep to these rules, and one draw needn't show every extreme that they name: `query`: every entry lies within the range; entries of one row may be alike in size or sign across heads. A permutation of 0 to 32767. Number the rows i = h * 64 * 128 + g * 128 + r with r below 128, and take the rows of one g in the order of h and then r: the first 256 of them hold consecutive positions from b * 256 on, the last 256 consecutive positions from (127 - b) * 256 on, for a b that differs from g to g.
All inputs are finite; a program needn't handle non-finite values.
Results may differ from the reference program's by a relative error of at most 0.022.
Values may be sent and summed in bfloat16 or wider, within the bound.
No kernel may reach another device: no remote copies, remote signals or barrier semaphores. Data moves between devices by JAX's collectives and lax.ppermute only.
A program may use at most 128 MiB of HBM per device.

```python
import math
import jax
import jax.numpy as jnp
from jax import lax

QUERY_HEADS = 32
KEY_VALUE_HEADS = 4
HEAD_DIMENSION = 128
INNER_STEPS = 3
GROUP_ROWS = 512
PAIR_GROUP_COUNT = 64
WINDOW_GROUPS = 5
PIECE = 128
BLOCK = 256
SEQUENCE_LENGTH = 32768
N_HEAD = 4
N_OUTER = 8


def draw_query(key, part):
    key = jax.random.fold_in(key, 11)
    array_extent = (SEQUENCE_LENGTH, KEY_VALUE_HEADS, QUERY_HEADS // KEY_VALUE_HEADS, HEAD_DIMENSION)
    base_offset = jnp.clip(jax.random.normal(key, array_extent, jnp.float32), -4.5, 4.5)
    return base_offset.reshape(SEQUENCE_LENGTH, QUERY_HEADS * HEAD_DIMENSION).astype(jnp.bfloat16)


def draw_key_value(key, part):
    key = jax.random.fold_in(key, 23)
    array_extent = (SEQUENCE_LENGTH, KEY_VALUE_HEADS, 2, HEAD_DIMENSION)
    base_offset = jnp.clip(jax.random.normal(key, array_extent, jnp.float32), -4.5, 4.5)
    return base_offset.reshape(SEQUENCE_LENGTH, 2 * KEY_VALUE_HEADS * HEAD_DIMENSION).astype(jnp.bfloat16)


def draw_positions(key, part):
    key = jax.random.fold_in(key, 37)
    order = jax.random.permutation(key, PAIR_GROUP_COUNT).astype(jnp.int32)
    index = jnp.arange(SEQUENCE_LENGTH, dtype=jnp.int32)
    head_part = index // (PAIR_GROUP_COUNT * PIECE)
    member = index // PIECE % PAIR_GROUP_COUNT
    within = index % PIECE
    local = head_part * PIECE + within
    paired = order[member]
    first = paired * BLOCK + local
    second = (2 * PAIR_GROUP_COUNT - 1 - paired) * BLOCK + (local - BLOCK)
    return jnp.where(local < BLOCK, first, second).astype(jnp.int32)


def block_levels(rng, dims, cuts, least, top_value):
    loudness, own = 1.0, jax.random.fold_in(rng, 6)
    for axis_at, shards_of in cuts:
        draws = jnp.exp(jax.random.uniform(jax.random.fold_in(own, axis_at), (shards_of,), jnp.float32, least / len(cuts), top_value / len(cuts)))
        loudness = loudness * jnp.repeat(draws, dims[axis_at] // shards_of).reshape([-1 if axis == axis_at else 1 for axis in range(len(dims))])
    return loudness


def noise(rng, shape, width, limit, shards=(), held_as=jnp.bfloat16):
    drawn = jax.random.normal(rng, shape, jnp.float32) * width
    if len(shards) > 0:
        drawn = block_levels(rng, shape, shards, -0.22, 0.18) * drawn
    return jnp.clip(drawn, min=-limit, max=limit).astype(held_as)


def setup_inputs(seed: int = 0) -> dict:
    seeds = jax.random.split(jax.random.key(seed), 5)
    query = draw_query(jax.random.fold_in(seeds[4], 71), 0)
    key_value = draw_key_value(jax.random.fold_in(seeds[4], 71), 0)
    grad_out = noise(seeds[2], (SEQUENCE_LENGTH, QUERY_HEADS * HEAD_DIMENSION), 1.0, 6.0, ((0, 256),))
    positions = draw_positions(jax.random.fold_in(seeds[4], 71), 0)
    return {"query": query, "key_value": key_value, "grad_out": grad_out, "positions": positions}


def by_group(values):
    cols = values.shape[1]
    return jnp.transpose(values.reshape(N_HEAD, PAIR_GROUP_COUNT, PIECE, cols), (1, 0, 2, 3)).reshape(PAIR_GROUP_COUNT, GROUP_ROWS, cols)

def by_row(values):
    cols = values.shape[2]
    return jnp.transpose(values.reshape(PAIR_GROUP_COUNT, N_HEAD, PIECE, cols), (1, 0, 2, 3)).reshape(SEQUENCE_LENGTH, cols)

def reference(query, key_value, grad_out, positions):
    scale = 1.0 / math.sqrt(HEAD_DIMENSION)
    group_index = QUERY_HEADS // KEY_VALUE_HEADS
    query_groups = by_group(query)
    inner_outer_groups = by_group(key_value)
    grad_groups = by_group(grad_out)
    pos_groups = by_group(positions.reshape(SEQUENCE_LENGTH, 1))[:, :, 0]
    offsets = jnp.array([s * N_OUTER for s in range(INNER_STEPS + 1)] + [1], dtype=jnp.int32)

    def step(dkv, index):
        selected_index = ((index - offsets) % PAIR_GROUP_COUNT).astype(jnp.int32)
        q_rows = query_groups[index]
        g_rows = grad_groups[index]
        q_pos = pos_groups[index]
        k_pos = pos_groups[selected_index].reshape(WINDOW_GROUPS * GROUP_ROWS)
        window_pairs = inner_outer_groups[selected_index].reshape(WINDOW_GROUPS * GROUP_ROWS, 2 * KEY_VALUE_HEADS * HEAD_DIMENSION)
        visible = k_pos[None, None, :] <= q_pos[None, :, None]
        out_cols = []
        dq_cols = []
        key_value_gradient_columns = []
        for head_index in range(KEY_VALUE_HEADS):
            q_float = q_rows[:, head_index * group_index * HEAD_DIMENSION:(head_index + 1) * group_index * HEAD_DIMENSION].reshape(GROUP_ROWS, group_index, HEAD_DIMENSION).astype(jnp.float32)
            g_float = jnp.transpose(g_rows[:, head_index * group_index * HEAD_DIMENSION:(head_index + 1) * group_index * HEAD_DIMENSION].reshape(GROUP_ROWS, group_index, HEAD_DIMENSION).astype(jnp.float32), (1, 0, 2))
            keys = window_pairs[:, head_index * 2 * HEAD_DIMENSION:head_index * 2 * HEAD_DIMENSION + HEAD_DIMENSION].astype(jnp.float32)
            values = window_pairs[:, head_index * 2 * HEAD_DIMENSION + HEAD_DIMENSION:(head_index + 1) * 2 * HEAD_DIMENSION].astype(jnp.float32)
            scores = jnp.einsum('rhd,nd->hrn', q_float, keys) * scale
            masked = jnp.where(visible, scores, -1e+30)
            top = lax.optimization_barrier(jnp.max(masked, axis=-1, keepdims=True))
            weights = jnp.where(visible, jnp.exp(masked - top), 0.0)
            total = lax.optimization_barrier(jnp.sum(weights, axis=-1))
            rounded = lax.optimization_barrier(weights.astype(jnp.bfloat16)).astype(jnp.float32)
            summed = jnp.einsum('hrn,nd->hrd', rounded, values)
            outputs = (summed / total[..., None]).astype(jnp.bfloat16)
            lse = top[..., 0] + jnp.log(total)
            delta = lax.optimization_barrier(jnp.sum(g_float * outputs.astype(jnp.float32), axis=-1))
            probs = jnp.where(visible, jnp.exp(masked - lse[..., None]), 0.0)
            probs_low = lax.optimization_barrier(probs.astype(jnp.bfloat16)).astype(jnp.float32)
            dprob = jnp.einsum('hrd,nd->hrn', g_float, values)
            dscore = lax.optimization_barrier((probs * (dprob - delta[..., None])).astype(jnp.bfloat16)).astype(jnp.float32)
            dquery = (jnp.einsum('hrn,nd->rhd', dscore, keys) * scale).astype(jnp.bfloat16)
            dkey = jnp.einsum('hrn,rhd->nd', dscore, q_float) * scale
            dvalue = jnp.einsum('hrn,hrd->nd', probs_low, g_float)
            out_cols.append(jnp.transpose(outputs, (1, 0, 2)).reshape(GROUP_ROWS, group_index * HEAD_DIMENSION))
            dq_cols.append(dquery.reshape(GROUP_ROWS, group_index * HEAD_DIMENSION))
            key_value_gradient_columns.append(jnp.concatenate([dkey, dvalue], axis=1))
        summand_terms = jnp.concatenate(key_value_gradient_columns, axis=1).reshape(WINDOW_GROUPS, GROUP_ROWS, 2 * KEY_VALUE_HEADS * HEAD_DIMENSION)
        dkv = dkv.at[selected_index].add(summand_terms)
        return (dkv, (jnp.concatenate(out_cols, axis=1), jnp.concatenate(dq_cols, axis=1)))
    start_position = jnp.zeros((PAIR_GROUP_COUNT, GROUP_ROWS, 2 * KEY_VALUE_HEADS * HEAD_DIMENSION), jnp.float32)
    dkv, (out_groups, dq_groups) = lax.scan(step, start_position, jnp.arange(PAIR_GROUP_COUNT, dtype=jnp.int32))
    return (by_row(out_groups), by_row(dq_groups), by_row(dkv))
```

```python
import math

import jax
import jax.numpy as jnp
from jax import lax
from jax.experimental import pallas as pl
from jax.experimental.pallas import tpu as pltpu
from jax.sharding import PartitionSpec as P

D = 128
PIECE = 128
HALF = 256
ROWS = 512
HEADER = 16
BLOCKS = 128
INNER_STEPS = 3
SCALE = 1.0 / math.sqrt(D)
EXP2_SCALE = SCALE * math.log2(math.e)
VMEM_LIMIT = 48 * 2**20
f32, bf16 = jnp.float32, jnp.bfloat16
NT = (((1,), (1,)), ((), ()))
NN = (((1,), (0,)), ((), ()))


def dot(a, b, dims):
    return lax.dot_general(a, b, dims, preferred_element_type=f32)


def places(h, pay_refs):
    found = []
    for ref in pay_refs:
        b = jnp.max(ref[ROWS : ROWS + HEADER, :].astype(f32)).astype(jnp.int32)
        swapped = jnp.where(b < BLOCKS // 2, 0, 1) ^ (h // 2)
        early = pl.multiple_of(swapped * HALF, HALF)
        found.append((jnp.minimum(b, BLOCKS - 1 - b), early, pl.multiple_of(HALF - early, HALF)))
    return found


def causal(h):
    def position(axis):
        row = lax.broadcasted_iota(jnp.int32, (HALF, HALF), axis)
        return jnp.where(h % 2 == 0, row, (row + PIECE) % HALF)

    return position(0) <= position(1)


def join(pieces, joined):
    for k, piece in enumerate(pieces):
        joined[k * PIECE : (k + 1) * PIECE, :] = piece[...]


def fwd_kernel(h_ref, q0, q1, q2, q3, g0, g1, g2, g3, own, w1, w2, w3, w4,
               o0, o1, o2, o3, q_out, ga_ref, wo_ref, ww_ref, vt_ref, s_ref, g_ref, o_ref):
    h = h_ref[0]
    pays = [own, w1, w2, w3, w4]
    place = places(h, pays)
    b_own, q_early, q_late = place[0]

    @pl.when(pl.program_id(0) == 0)
    def _():
        for i, ref in enumerate(pays):
            for half in range(2):
                vt_ref[i, half] = jnp.transpose(ref[half * HALF : (half + 1) * HALF, D:], (1, 0))

    join((q0, q1, q2, q3), q_out)
    join((g0, g1, g2, g3), g_ref)
    mask = causal(h)
    is_early = [None] + [place[w][0] < b_own for w in range(1, 5)]
    tops = []

    def score(n, group, key_row, query_row, masked=False):
        s = dot(pays[group][pl.ds(key_row, HALF), :D], q_out[pl.ds(query_row, HALF), :], NT)
        if masked:
            s = jnp.where(mask, s, -1e30)
        s_ref[n] = s
        tops.append(jnp.max(s, axis=0, keepdims=True))

    score(0, 0, q_early, q_early, True)
    score(1, 0, q_early, q_late)
    score(2, 0, q_late, q_late, True)
    rows = [None]
    for w in range(1, 5):
        _, k_early, k_late = place[w]
        key_row = pl.multiple_of(jnp.where(is_early[w], k_early, k_late), HALF)
        query_row = pl.multiple_of(jnp.where(is_early[w], q_early, q_late), HALF)
        rows.append(key_row)
        score(1 + 2 * w, w, k_early, q_late)
        score(2 + 2 * w, w, key_row, query_row)
    m_early, m_late = tops[0], jnp.maximum(tops[1], tops[2])
    for w in range(1, 5):
        m_late = jnp.maximum(m_late, tops[1 + 2 * w])
        top = tops[2 + 2 * w]
        m_early = jnp.where(is_early[w], jnp.maximum(m_early, top), m_early)
        m_late = jnp.where(is_early[w], m_late, jnp.maximum(m_late, top))

    def weigh(n, m):
        wt = jnp.exp2((s_ref[n] - m) * EXP2_SCALE)
        return wt.astype(bf16), jnp.sum(wt, axis=0, keepdims=True)

    def values(group, row):
        return vt_ref[group, row // HALF]

    wt, l_early = weigh(0, m_early)
    wo_ref[0, 0] = wt
    a_early = dot(values(0, q_early), wt, NN)
    wt, l_late = weigh(1, m_late)
    wo_ref[0, 1] = wt
    a_late = dot(values(0, q_early), wt, NN)
    wt, l = weigh(2, m_late)
    wo_ref[0, 2] = wt
    a_late += dot(values(0, q_late), wt, NN)
    l_late += l
    for w in range(1, 5):
        wt, l = weigh(1 + 2 * w, m_late)
        ww_ref[0, w - 1, 0] = wt
        a_late += dot(values(w, place[w][1]), wt, NN)
        l_late += l
        wt, l = weigh(2 + 2 * w, jnp.where(is_early[w], m_early, m_late))
        ww_ref[0, w - 1, 1] = wt
        a = dot(values(w, rows[w]), wt, NN)
        a_early += jnp.where(is_early[w], a, 0.0)
        a_late += jnp.where(is_early[w], 0.0, a)
        l_early += jnp.where(is_early[w], l, 0.0)
        l_late += jnp.where(is_early[w], 0.0, l)
    for row, a, l in ((q_early, a_early, l_early), (q_late, a_late, l_late)):
        r = 1.0 / l
        out = jnp.transpose(a * r, (1, 0)).astype(bf16)
        r_rows = jnp.transpose(jnp.broadcast_to(r, (D, HALF)), (1, 0))
        o_ref[pl.ds(row, HALF), :] = out
        g = g_ref[pl.ds(row, HALF), :].astype(f32) * r_rows
        ga_ref[pl.ds(row, HALF), :D] = g.astype(bf16)
        ga_ref[pl.ds(row, HALF), D:] = (-g * out.astype(f32)).astype(bf16)
    for k, ref in enumerate((o0, o1, o2, o3)):
        ref[...] = o_ref[k * PIECE : (k + 1) * PIECE, :]


def forward(h, q, g, pays):
    heads = q[0].shape[1] // D
    piece = pl.BlockSpec((PIECE, D), lambda j, h: (0, j))
    pay = pl.BlockSpec(pays[0].shape, lambda j, h: (0, 0))
    wo_spec = pl.BlockSpec((1, 3, HALF, HALF), lambda j, h: (j, 0, 0, 0))
    ww_spec = pl.BlockSpec((1, 4, 2, HALF, HALF), lambda j, h: (j, 0, 0, 0, 0))
    return pl.pallas_call(
        fwd_kernel,
        grid_spec=pltpu.PrefetchScalarGridSpec(
            num_scalar_prefetch=1,
            grid=(heads,),
            in_specs=[piece] * 8 + [pay] * 5,
            out_specs=[piece] * 4 + [
                pl.BlockSpec((ROWS, D), lambda j, h: (0, j)),
                pl.BlockSpec((ROWS, 2 * D), lambda j, h: (0, j)),
                wo_spec, ww_spec],
            scratch_shapes=[
                pltpu.VMEM((5, 2, D, HALF), bf16),
                pltpu.VMEM((11, HALF, HALF), f32),
                pltpu.VMEM((ROWS, D), bf16),
                pltpu.VMEM((ROWS, D), bf16),
            ],
        ),
        out_shape=[jax.ShapeDtypeStruct((PIECE, heads * D), bf16)] * 4 + [
            jax.ShapeDtypeStruct((ROWS, heads * D), bf16),
            jax.ShapeDtypeStruct((ROWS, heads * 2 * D), bf16),
            jax.ShapeDtypeStruct((heads, 3, HALF, HALF), bf16),
            jax.ShapeDtypeStruct((heads, 4, 2, HALF, HALF), bf16),
        ],
        compiler_params=pltpu.CompilerParams(vmem_limit_bytes=VMEM_LIMIT),
        cost_estimate=pl.CostEstimate(
            flops=heads * 11 * 4 * HALF * HALF * D, bytes_accessed=16 * 2**20,
            transcendentals=heads * 11 * HALF * HALF),
        name="forward",
    )(h, *q, *g, *pays)


def bwd_kernel(h_ref, q_ref, ga_ref, own, w1, w2, w3, w4, wo_ref, ww_ref,
               d0, d1, d2, d3, t_ref, kt_ref, va_ref, acc_ref, d_ref):
    h = h_ref[0]
    pays = [own, w1, w2, w3, w4]
    place = places(h, pays)
    b_own, q_early, q_late = place[0]
    j = pl.program_id(0)

    @pl.when(j == 0)
    def _():
        for i, ref in enumerate(pays):
            for half in range(2):
                kt_ref[i, half] = jnp.transpose(ref[half * HALF : (half + 1) * HALF, :D], (1, 0))
            va_ref[i, :, :D] = ref[:ROWS, D:]
            va_ref[i, :, D:] = jnp.ones((ROWS, D), bf16)
        acc_ref[...] = jnp.zeros_like(acc_ref)

    is_early = [None] + [place[w][0] < b_own for w in range(1, 5)]

    def block(group, key_row, query_row, wt):
        ga = ga_ref[pl.ds(query_row, HALF), :]
        dp = dot(va_ref[group, pl.ds(key_row, HALF), :], ga, NT)
        ds = (wt.astype(f32) * dp).astype(bf16)
        acc_ref[group, pl.ds(key_row, HALF), D:] += dot(wt, ga[:, :D], NN)
        acc_ref[group, pl.ds(key_row, HALF), :D] += dot(ds, q_ref[pl.ds(query_row, HALF), :], NN)
        return dot(kt_ref[group, key_row // HALF], ds, NN)

    d_early = block(0, q_early, q_early, wo_ref[0, 0])
    d_late = block(0, q_early, q_late, wo_ref[0, 1])
    d_late += block(0, q_late, q_late, wo_ref[0, 2])
    for w in range(1, 5):
        _, k_early, k_late = place[w]
        key_row = pl.multiple_of(jnp.where(is_early[w], k_early, k_late), HALF)
        query_row = pl.multiple_of(jnp.where(is_early[w], q_early, q_late), HALF)
        d_late += block(w, k_early, q_late, ww_ref[0, w - 1, 0])
        d = block(w, key_row, query_row, ww_ref[0, w - 1, 1])
        d_early += jnp.where(is_early[w], d, 0.0)
        d_late += jnp.where(is_early[w], 0.0, d)
    for row, d in ((q_early, d_early), (q_late, d_late)):
        d_ref[pl.ds(row, HALF), :] = jnp.transpose(d * SCALE, (1, 0)).astype(bf16)
    for k, ref in enumerate((d0, d1, d2, d3)):
        ref[...] = d_ref[k * PIECE : (k + 1) * PIECE, :]

    @pl.when(j == pl.num_programs(0) - 1)
    def _():
        for i in range(5):
            t_ref[i, :, :D] = (acc_ref[i, :, :D] * SCALE).astype(t_ref.dtype)
            t_ref[i, :, D:] = acc_ref[i, :, D:].astype(t_ref.dtype)


def backward(h, q, ga, pays, wo, ww):
    heads = q.shape[1] // D
    piece = pl.BlockSpec((PIECE, D), lambda j, h: (0, j))
    pay = pl.BlockSpec(pays[0].shape, lambda j, h: (0, 0))
    return pl.pallas_call(
        bwd_kernel,
        grid_spec=pltpu.PrefetchScalarGridSpec(
            num_scalar_prefetch=1,
            grid=(heads,),
            in_specs=[
                pl.BlockSpec((ROWS, D), lambda j, h: (0, j)),
                pl.BlockSpec((ROWS, 2 * D), lambda j, h: (0, j)),
            ] + [pay] * 5 + [
                pl.BlockSpec((1, 3, HALF, HALF), lambda j, h: (j, 0, 0, 0)),
                pl.BlockSpec((1, 4, 2, HALF, HALF), lambda j, h: (j, 0, 0, 0, 0)),
            ],
            out_specs=[piece] * 4 + [pl.BlockSpec((5, ROWS, 2 * D), lambda j, h: (0, 0, 0))],
            scratch_shapes=[
                pltpu.VMEM((5, 2, D, HALF), bf16),
                pltpu.VMEM((5, ROWS, 2 * D), bf16),
                pltpu.VMEM((5, ROWS, 2 * D), f32),
                pltpu.VMEM((ROWS, D), bf16),
            ],
        ),
        out_shape=[jax.ShapeDtypeStruct((PIECE, heads * D), bf16)] * 4 + [
            jax.ShapeDtypeStruct((5, ROWS, 2 * D), bf16)],
        compiler_params=pltpu.CompilerParams(vmem_limit_bytes=VMEM_LIMIT),
        cost_estimate=pl.CostEstimate(
            flops=heads * 11 * 8 * HALF * HALF * D, bytes_accessed=16 * 2**20, transcendentals=0),
        name="backward",
    )(h, q, ga, *pays, wo, ww)


def place_kernel(h_ref, p0, p1, p2, p3, out, sems):
    h = h_ref[0]
    width = p0.shape[1]
    copies = []
    for k, piece in enumerate((p0, p1, p2, p3)):
        column = pl.multiple_of((h ^ k) * width, width)
        copies.append(pltpu.make_async_copy(piece, out.at[:, pl.ds(column, width)], sems.at[k]))
    for copy in copies:
        copy.start()
    for copy in copies:
        copy.wait()


def placed(h, pieces):
    rows, width = pieces[0].shape
    return pl.pallas_call(
        place_kernel,
        in_specs=[pl.BlockSpec(memory_space=pltpu.SMEM)] + [pl.BlockSpec(memory_space=pl.ANY)] * 4,
        out_specs=pl.BlockSpec(memory_space=pl.ANY),
        out_shape=jax.ShapeDtypeStruct((rows, 4 * width), pieces[0].dtype),
        scratch_shapes=[pltpu.SemaphoreType.DMA((4,))],
        name="place",
    )(h, *pieces)


def swap(x, k):
    return lax.ppermute(x, "head", [(i, i ^ k) for i in range(4)])


def along(x, axis, distance):
    n = lax.axis_size(axis)
    return lax.ppermute(x, axis, [(i, (i + distance) % n) for i in range(n)])


def columns(h, x, k):
    width = x.shape[1] // 4
    return lax.dynamic_slice(x, (0, (h ^ k) * width), (x.shape[0], width))


def to_heads(h, x):
    return [columns(h, x, 0)] + [swap(columns(h, x, k), k) for k in (1, 2, 3)]


def from_heads(pieces):
    return [pieces[0]] + [swap(pieces[k], k) for k in (1, 2, 3)]


def local(query, key_value, grad_out, positions):
    h = lax.axis_index("head")
    h_arg = jnp.full((1,), h, jnp.int32)
    block = positions[0] // HALF
    b = jnp.where(h < 2, block, BLOCKS - 1 - block)
    header = jnp.broadcast_to(b.astype(bf16), (HEADER, 2 * D))
    own = jnp.concatenate(to_heads(h, key_value) + [header], axis=0)
    w1 = along(own, "inner", 1)
    before = along(own, ("inner", "outer"), 1)
    q = to_heads(h, query)
    w2 = along(w1, "inner", 1)
    g = to_heads(h, grad_out)
    w3 = along(w2, "inner", 1)
    pays = [own, w1, w2, w3, before]
    *out, q_rows, ga, wo, ww = forward(h_arg, q, g, pays)
    out = from_heads(out)
    *dq, terms = backward(h_arg, q_rows, ga, pays, wo, ww)
    back = along(terms[4], ("inner", "outer"), -1)
    total = along(terms[3], "inner", -1)
    for step in (2, 1):
        total = (total.astype(f32) + terms[step].astype(f32)).astype(bf16)
        total = along(total, "inner", -1)
    dkv = (terms[0].astype(f32) + total.astype(f32) + back.astype(f32)).astype(bf16)
    dq = from_heads(dq)
    dkv = from_heads([dkv[k * PIECE : (k + 1) * PIECE] for k in range(4)])
    return placed(h_arg, out), placed(h_arg, dq), placed(h_arg, dkv).astype(f32)


def solution(mesh):
    spec = P(("head", "inner", "outer"), None)
    return jax.shard_map(
        local,
        mesh=mesh,
        in_specs=(spec, spec, spec, P(("head", "inner", "outer"))),
        out_specs=(spec, spec, spec),
        check_vma=False,
    )
```

```python
import functools
import math

import jax
import jax.numpy as jnp
from jax import lax
from jax.experimental import pallas as pl
from jax.experimental.pallas import tpu as pltpu
from jax.sharding import PartitionSpec as P

D = 128
PIECE = 128
HALF = 256
ROWS = 512
HEADER = 16
BLOCKS = 128
SCALE = 1.0 / math.sqrt(D)
EXP2_SCALE = SCALE * math.log2(math.e)
VMEM_LIMIT = 48 * 2**20
f32, bf16 = jnp.float32, jnp.bfloat16
NT = (((1,), (1,)), ((), ()))
NN = (((1,), (0,)), ((), ()))
SUMS = 16


def dot(a, b, dims):
    return lax.dot_general(a, b, dims, preferred_element_type=f32)


def place(h, ref):
    b = jnp.max(ref[ROWS : ROWS + HEADER, :].astype(f32)).astype(jnp.int32)
    swapped = jnp.where(b < BLOCKS // 2, 0, 1) ^ (h // 2)
    early = pl.multiple_of(swapped * HALF, HALF)
    return jnp.minimum(b, BLOCKS - 1 - b), early, pl.multiple_of(HALF - early, HALF)


def causal(h):
    def position(axis):
        row = lax.broadcasted_iota(jnp.int32, (HALF, HALF), axis)
        return jnp.where(h % 2 == 0, row, (row + PIECE) % HALF)

    return position(0) <= position(1)


class Layout:
    def __init__(self, h, own_ref, windows, with_own):
        self.b, self.q_early, self.q_late = place(h, own_ref)
        self.blocks, self.spots = [], []
        if with_own:
            self.spots += [(0, 0), (0, 1), (0, 2)]
            self.blocks += [
                (own_ref, self.q_early, self.q_early, True, True),
                (own_ref, self.q_early, self.q_late, False, False),
                (own_ref, self.q_late, self.q_late, False, True),
            ]
        for group, ref in enumerate(windows):
            self.spots += [(group + with_own, 0), (group + with_own, 1)]
            b, k_early, k_late = place(h, ref)
            first = b < self.b
            key_row = pl.multiple_of(jnp.where(first, k_early, k_late), HALF)
            query_row = pl.multiple_of(jnp.where(first, self.q_early, self.q_late), HALF)
            self.blocks += [
                (ref, k_early, self.q_late, False, False),
                (ref, key_row, query_row, first, False),
            ]


def split(flag, x):
    if flag is True:
        return x, None
    if flag is False:
        return None, x
    return jnp.where(flag, x, 0.0), jnp.where(flag, 0.0, x)


def add(total, x):
    return total if x is None else x if total is None else total + x


STRIP = 64


def at(refs, layout, a, n):
    group, index = layout.spots[n]
    return refs[group].at[a, index]


def cols(ref, row, n, head):
    return ref[pl.ds(row, n), head * D : (head + 1) * D]


def weigh_blocks(layout, heads, q_ref, mask, vt_ref, s_ref, w_refs, old):
    tops = [[None, None] if old is None else list(old[a]) for a in range(heads)]
    for a in range(heads):
        for n, (keys, key_row, query_row, first, masked) in enumerate(layout.blocks):
            s = dot(keys[pl.ds(key_row, HALF), :D], cols(q_ref, query_row, HALF, a), NT)
            if masked:
                s = jnp.where(mask, s, -1e30)
            s_ref[a, n] = s
            top = jnp.max(s, axis=0, keepdims=True)
            for half in range(2):
                if first is (half == 1):
                    continue
                t = top
                if first is not True and first is not False:
                    t = jnp.where(first if half == 0 else jnp.logical_not(first), top, -1e30)
                tops[a][half] = t if tops[a][half] is None else jnp.maximum(tops[a][half], t)
    acc = [[None, None] for _ in range(heads)]
    for a in range(heads):
        for n, (keys, key_row, query_row, first, masked) in enumerate(layout.blocks):
            if first is True:
                m = tops[a][0]
            elif first is False:
                m = tops[a][1]
            else:
                m = jnp.where(first, tops[a][0], tops[a][1])
            w_ref = at(w_refs, layout, a, n)
            for r in range(0, HALF, STRIP):
                x = s_ref[a, n, r : r + STRIP, :]
                w_ref[r : r + STRIP, :] = jnp.exp2((x - m) * EXP2_SCALE).astype(bf16)
            for half, x in enumerate(split(first, dot(vt_ref[n], w_ref[...], NN))):
                acc[a][half] = add(acc[a][half], x)
    return tops, acc


def load_vt(layout, vt_ref):
    @pl.when(pl.program_id(0) == 0)
    def _():
        for n, (keys, key_row, *_) in enumerate(layout.blocks):
            vt_ref[n, :D, :] = jnp.transpose(keys[pl.ds(key_row, HALF), D:], (1, 0))
            vt_ref[n, D:, :] = jnp.ones((SUMS, HALF), bf16)


def fwd_first_kernel(heads, h_ref, q0, q1, q2, q3, own, *refs):
    n_win = (len(refs) - 6) // 2
    windows, refs = refs[:n_win], refs[n_win:]
    w_refs = refs[3 : 4 + n_win]
    q_out, state_ref, top_ref = refs[:3]
    vt_ref, s_ref = refs[4 + n_win :]
    h = h_ref[0]
    layout = Layout(h, own, windows, True)
    load_vt(layout, vt_ref)
    for k, piece in enumerate((q0, q1, q2, q3)):
        q_out[k * PIECE : (k + 1) * PIECE, :] = piece[...]
    tops, acc = weigh_blocks(layout, heads, q_out, causal(h), vt_ref, s_ref, w_refs, None)
    for a in range(heads):
        for half in range(2):
            state_ref[a, half] = acc[a][half]
            top_ref[a, half] = jnp.broadcast_to(tops[a][half], (8, HALF))


def fwd_last_kernel(heads, h_ref, q_ref, g0, g1, g2, g3, own, win, state_in, top_in,
                    o0, o1, o2, o3, g_out, gb_out, w_ref, vt_ref, s_ref, g_ref, o_ref):
    h = h_ref[0]
    layout = Layout(h, own, [win], False)
    load_vt(layout, vt_ref)
    for k, piece in enumerate((g0, g1, g2, g3)):
        g_ref[k * PIECE : (k + 1) * PIECE, :] = piece[...]
    old = [[top_in[a, half, :1, :] for half in range(2)] for a in range(heads)]
    tops, acc = weigh_blocks(layout, heads, q_ref, None, vt_ref, s_ref, [w_ref], old)
    for a in range(heads):
        for half, row in enumerate((layout.q_early, layout.q_late)):
            shrink = jnp.exp2((old[a][half] - tops[a][half]) * EXP2_SCALE)
            t = state_in[a, half] * shrink + acc[a][half]
            r = 1.0 / t[D : D + 1]
            out = jnp.transpose(t[:D] * r, (1, 0)).astype(bf16)
            o_ref[pl.ds(row, HALF), a * D : (a + 1) * D] = out
            g = cols(g_ref, row, HALF, a).astype(f32)
            for ref, factor in ((g_out, r * shrink), (gb_out, r)):
                scaled = g * jnp.transpose(jnp.broadcast_to(factor, (D, HALF)), (1, 0))
                ref[pl.ds(row, HALF), 2 * a * D : (2 * a + 1) * D] = scaled.astype(bf16)
                ref[pl.ds(row, HALF), (2 * a + 1) * D : (2 * a + 2) * D] = (
                    -scaled * out.astype(f32)).astype(bf16)
    for k, ref in enumerate((o0, o1, o2, o3)):
        ref[...] = o_ref[k * PIECE : (k + 1) * PIECE, :]


PAY_SPEC = pl.BlockSpec((ROWS + HEADER, 2 * D), lambda j, h: (0, 0))


def piece_spec(heads):
    return pl.BlockSpec((PIECE, heads * D), lambda j, h: (0, j))


def rows_spec(heads):
    return pl.BlockSpec((ROWS, heads * D), lambda j, h: (0, j))


def w_spec(heads, n):
    return pl.BlockSpec((heads, n, HALF, HALF), lambda j, h: (j, 0, 0, 0))


def half_spec(heads, n):
    return pl.BlockSpec((heads, 2, n, HALF), lambda j, h: (j, 0, 0, 0))


def call(kernel, name, steps, ins, in_specs, outs, out_specs, scratch, flops, exps=0):
    return pl.pallas_call(
        kernel,
        grid_spec=pltpu.PrefetchScalarGridSpec(
            num_scalar_prefetch=1, grid=(steps,), in_specs=in_specs, out_specs=out_specs,
            scratch_shapes=scratch),
        out_shape=outs,
        compiler_params=pltpu.CompilerParams(vmem_limit_bytes=VMEM_LIMIT),
        cost_estimate=pl.CostEstimate(flops=flops, bytes_accessed=8 * 2**20, transcendentals=exps),
        name=name,
    )(*ins)


def shape(*dims, dtype=bf16):
    return jax.ShapeDtypeStruct(dims, dtype)


STEP_FIRST, STEP_LAST, STEP_A, STEP_B, STEP_C = 2, 4, 8, 2, 2


def forward_first(h, q, own, windows):
    heads = q[0].shape[1] // D
    n = 3 + 2 * len(windows)
    e = STEP_FIRST
    return call(
        functools.partial(fwd_first_kernel, e), "forward_first", heads // e, (h, *q, own, *windows),
        [piece_spec(e)] * 4 + [PAY_SPEC] * (1 + len(windows)),
        [shape(ROWS, heads * D), shape(heads, 2, D + SUMS, HALF, dtype=f32),
         shape(heads, 2, 8, HALF, dtype=f32), shape(heads, 3, HALF, HALF)]
        + [shape(heads, 2, HALF, HALF)] * len(windows),
        [rows_spec(e), half_spec(e, D + SUMS), half_spec(e, 8), w_spec(e, 3)]
        + [w_spec(e, 2)] * len(windows),
        [pltpu.VMEM((n, D + SUMS, HALF), bf16), pltpu.VMEM((e, n, HALF, HALF), f32)],
        heads * n * 4 * HALF * HALF * D, heads * n * HALF * HALF)


def forward_last(h, q_rows, g, own, window, state, top):
    heads = q_rows.shape[1] // D
    e = STEP_LAST
    return call(
        functools.partial(fwd_last_kernel, e), "forward_last", heads // e,
        (h, q_rows, *g, own, window, state, top),
        [rows_spec(e)] + [piece_spec(e)] * 4 + [PAY_SPEC] * 2 + [half_spec(e, D + SUMS), half_spec(e, 8)],
        [shape(PIECE, heads * D)] * 4 + [shape(ROWS, heads * 2 * D)] * 2 + [shape(heads, 2, HALF, HALF)],
        [piece_spec(e)] * 4 + [rows_spec(2 * e)] * 2 + [w_spec(e, 2)],
        [pltpu.VMEM((2, D + SUMS, HALF), bf16), pltpu.VMEM((e, 2, HALF, HALF), f32),
         pltpu.VMEM((ROWS, e * D), bf16), pltpu.VMEM((ROWS, e * D), bf16)],
        heads * 2 * 4 * HALF * HALF * D, heads * 2 * HALF * HALF)


def bwd_kernel(heads, n_win, with_own, first, last, h_ref, q_ref, ga_ref, own, *refs):
    windows, refs = refs[:n_win], refs[n_win:]
    n_terms = n_win + with_own
    w_refs, refs = refs[:n_terms], refs[n_terms:]
    if not first:
        d_in, refs = refs[0], refs[1:]
    if last:
        d_outs, refs = refs[:4], refs[4:]
    else:
        d_out, refs = refs[0], refs[1:]
    terms, refs = refs[:n_terms], refs[n_terms:]
    kt_ref, va_ref, acc_ref, ds_ref = refs[:4]
    h = h_ref[0]
    layout = Layout(h, own, windows, with_own)
    j = pl.program_id(0)

    @pl.when(j == 0)
    def _():
        for n, (keys, key_row, *_) in enumerate(layout.blocks):
            kt_ref[n] = jnp.transpose(keys[pl.ds(key_row, HALF), :D], (1, 0))
            va_ref[n, :, :D] = keys[pl.ds(key_row, HALF), D:]
            va_ref[n, :, D:] = jnp.ones((HALF, D), bf16)
        acc_ref[...] = jnp.zeros_like(acc_ref)

    total = [[None, None] if first else [d_in[a, 0], d_in[a, 1]] for a in range(heads)]

    def grads(row, a, width):
        return ga_ref[pl.ds(row, HALF), 2 * a * D : (2 * a + width) * D]

    for n, (keys, key_row, query_row, early, masked) in enumerate(layout.blocks):
        for a in range(heads):
            dp = dot(va_ref[n], grads(query_row, a, 2), NT)
            ds_ref[a, n] = (at(w_refs, layout, a, n)[...].astype(f32) * dp).astype(bf16)
    for n, (keys, key_row, query_row, early, masked) in enumerate(layout.blocks):
        value_sum = key_sum = None
        for a in range(heads):
            value_sum = add(value_sum, dot(at(w_refs, layout, a, n)[...], grads(query_row, a, 1), NN))
            key_sum = add(key_sum, dot(ds_ref[a, n], cols(q_ref, query_row, HALF, a), NN))
            for half, x in enumerate(split(early, dot(kt_ref[n], ds_ref[a, n], NN))):
                total[a][half] = add(total[a][half], x)
        acc_ref[n, :, D:] += value_sum
        acc_ref[n, :, :D] += key_sum
    if last:
        d_ref = refs[4]
        for a in range(heads):
            for row, d in ((layout.q_early, total[a][0]), (layout.q_late, total[a][1])):
                d_ref[pl.ds(row, HALF), a * D : (a + 1) * D] = jnp.transpose(d * SCALE, (1, 0)).astype(bf16)
        for k, ref in enumerate(d_outs):
            ref[...] = d_ref[k * PIECE : (k + 1) * PIECE, :]
    else:
        for a in range(heads):
            for half in range(2):
                d_out[a, half] = total[a][half]

    @pl.when(j == pl.num_programs(0) - 1)
    def _():
        n = 0
        for term in terms:
            if with_own and n == 0:
                parts = [(layout.q_early, acc_ref[0] + acc_ref[1]), (layout.q_late, acc_ref[2])]
                n = 3
            else:
                flag = layout.blocks[n + 1][3]
                k_early = layout.blocks[n][1]
                x, y = acc_ref[n], acc_ref[n + 1]
                parts = [
                    (k_early, x + jnp.where(flag, y, 0.0)),
                    (pl.multiple_of(HALF - k_early, HALF), jnp.where(flag, 0.0, y)),
                ]
                n += 2
            for row, x in parts:
                term[pl.ds(row, HALF), :D] = (x[:, :D] * SCALE).astype(bf16)
                term[pl.ds(row, HALF), D:] = x[:, D:].astype(bf16)


def backward(name, e, h, q_rows, ga, own, windows, w, d=None, with_own=False, last=False):
    heads = q_rows.shape[1] // D
    n = 3 * with_own + 2 * len(windows)
    n_terms = with_own + len(windows)
    first = d is None
    return call(
        functools.partial(bwd_kernel, e, len(windows), with_own, first, last), name, heads // e,
        (h, q_rows, ga, own, *windows, *w) + (() if first else (d,)),
        [rows_spec(e), rows_spec(2 * e)] + [PAY_SPEC] * (1 + len(windows))
        + [w_spec(e, 3)] * with_own + [w_spec(e, 2)] * len(windows)
        + ([] if first else [half_spec(e, D)]),
        ([shape(PIECE, heads * D)] * 4 if last else [shape(heads, 2, D, HALF, dtype=f32)])
        + [shape(ROWS, 2 * D)] * n_terms,
        ([piece_spec(e)] * 4 if last else [half_spec(e, D)])
        + [pl.BlockSpec((ROWS, 2 * D), lambda j, h: (0, 0))] * n_terms,
        [pltpu.VMEM((n, D, HALF), bf16), pltpu.VMEM((n, HALF, 2 * D), bf16),
         pltpu.VMEM((n, HALF, 2 * D), f32), pltpu.VMEM((e, n, HALF, HALF), bf16)]
        + ([pltpu.VMEM((ROWS, e * D), bf16)] if last else []),
        heads * n * 8 * HALF * HALF * D)


def place_kernel(h_ref, p0, p1, p2, p3, out):
    width = p0.shape[1]
    for k, piece in enumerate((p0, p1, p2, p3)):
        column = pl.multiple_of((h_ref[0] ^ k) * width, width)
        out[:, pl.ds(column, width)] = piece[...].astype(out.dtype)


def placed(h, pieces, dtype=bf16):
    rows, width = pieces[0].shape
    return pl.pallas_call(
        place_kernel,
        in_specs=[pl.BlockSpec(memory_space=pltpu.SMEM)] + [pl.BlockSpec(memory_space=pltpu.VMEM)] * 4,
        out_specs=pl.BlockSpec(memory_space=pltpu.VMEM),
        out_shape=shape(rows, 4 * width, dtype=dtype),
        cost_estimate=pl.CostEstimate(flops=0, bytes_accessed=16 * rows * width, transcendentals=0),
        name="placed",
    )(h, *pieces)


def after(x, earlier):
    return lax.optimization_barrier((x, earlier))[0]


def swap(x, k):
    return lax.ppermute(x, "head", [(i, i ^ k) for i in range(4)])


def along(x, axis, distance):
    n = lax.axis_size(axis)
    return lax.ppermute(x, axis, [(i, (i + distance) % n) for i in range(n)])


def columns(h, x, k):
    width = x.shape[1] // 4
    return lax.dynamic_slice(x, (0, (h ^ k) * width), (x.shape[0], width))


def to_heads(h, x, earlier=None):
    pieces = [columns(h, x, k) for k in range(4)]
    if earlier is not None:
        pieces = pieces[:1] + [after(pieces[k], earlier[k]) for k in (1, 2, 3)]
    return from_heads(pieces)


def from_heads(pieces):
    return [pieces[0]] + [swap(pieces[k], k) for k in (1, 2, 3)]


def plus(x, y):
    return (x.astype(f32) + y.astype(f32)).astype(bf16)


def local(query, key_value, grad_out, positions):
    h = lax.axis_index("head")
    h_arg = jnp.full((1,), h, jnp.int32)
    block = positions[0] // HALF
    b = jnp.where(h < 2, block, BLOCKS - 1 - block)
    header = jnp.broadcast_to(b.astype(bf16), (HEADER, 2 * D))
    kv = to_heads(h, key_value)
    own = jnp.concatenate(kv + [header], axis=0)
    q = to_heads(h, query, kv)
    g = to_heads(h, grad_out, q)
    before = along(own, ("inner", "outer"), 1)
    w1 = along(own, "inner", 1)
    w2 = along(w1, "inner", 1)
    w3 = along(w2, "inner", 1)
    q_rows, state, top, wo, ww2, wwb, ww1 = forward_first(h_arg, q, own, [w2, before, w1])
    *out, ga, gb, ww3 = forward_last(h_arg, q_rows, g, own, w3, state, top)
    out = from_heads(out)
    d, t3 = backward("backward_a", STEP_A, h_arg, q_rows, gb, own, [w3], [ww3])
    s2 = along(t3, "inner", -1)
    d, t2, tb = backward("backward_b", STEP_B, h_arg, q_rows, ga, own, [w2, before], [ww2, wwb], d)
    s1 = along(plus(t2, s2), "inner", -1)
    back = along(tb, ("inner", "outer"), -1)
    *dq, t0, t1 = backward(
        "backward_c", STEP_C, h_arg, q_rows, ga, own, [w1], [wo, ww1], d, with_own=True, last=True)
    s0 = along(plus(t1, s1), "inner", -1)
    dq = from_heads(dq[:1] + [after(dq[k], out[k]) for k in (1, 2, 3)])
    dkv = (t0.astype(f32) + s0.astype(f32) + back.astype(f32)).astype(bf16)
    dkv = from_heads([dkv[k * PIECE : (k + 1) * PIECE] for k in range(4)])
    return placed(h_arg, out), placed(h_arg, dq), placed(h_arg, dkv, f32)


def solution(mesh):
    spec = P(("head", "inner", "outer"), None)
    return jax.shard_map(
        local,
        mesh=mesh,
        in_specs=(spec, spec, spec, P(("head", "inner", "outer"))),
        out_specs=(spec, spec, spec),
        check_vma=False,
    )
```

```python
import functools
import math

import jax
import jax.numpy as jnp
from jax import lax
from jax.experimental import pallas as pl
from jax.experimental.pallas import tpu as pltpu
from jax.sharding import PartitionSpec as P

D = 128
PIECE = 128
HALF = 256
ROWS = 512
HEADER = 16
BLOCKS = 128
SCALE = 1.0 / math.sqrt(D)
EXP2_SCALE = SCALE * math.log2(math.e)
VMEM_LIMIT = 26 * 2**20
f32, bf16 = jnp.float32, jnp.bfloat16
NT = (((1,), (1,)), ((), ()))
NN = (((1,), (0,)), ((), ()))
SUMS = 16


def dot(a, b, dims):
    return lax.dot_general(a, b, dims, preferred_element_type=f32)


def place(h, ref):
    b = jnp.max(ref[ROWS : ROWS + HEADER, :].astype(f32)).astype(jnp.int32)
    swapped = jnp.where(b < BLOCKS // 2, 0, 1) ^ (h // 2)
    early = pl.multiple_of(swapped * HALF, HALF)
    return jnp.minimum(b, BLOCKS - 1 - b), early, pl.multiple_of(HALF - early, HALF)


def causal(h):
    def position(axis):
        row = lax.broadcasted_iota(jnp.int32, (HALF, HALF), axis)
        return jnp.where(h % 2 == 0, row, (row + PIECE) % HALF)

    return position(0) <= position(1)


class Layout:
    def __init__(self, h, own_ref, windows, with_own):
        self.b, self.q_early, self.q_late = place(h, own_ref)
        self.blocks, self.spots = [], []
        if with_own:
            self.spots += [(0, 0), (0, 1), (0, 2)]
            self.blocks += [
                (own_ref, self.q_early, self.q_early, True, True),
                (own_ref, self.q_early, self.q_late, False, False),
                (own_ref, self.q_late, self.q_late, False, True),
            ]
        for group, ref in enumerate(windows):
            self.spots += [(group + with_own, 0), (group + with_own, 1)]
            b, k_early, k_late = place(h, ref)
            first = b < self.b
            key_row = pl.multiple_of(jnp.where(first, k_early, k_late), HALF)
            query_row = pl.multiple_of(jnp.where(first, self.q_early, self.q_late), HALF)
            self.blocks += [
                (ref, k_early, self.q_late, False, False),
                (ref, key_row, query_row, first, False),
            ]


def split(flag, x):
    if flag is True:
        return x, None
    if flag is False:
        return None, x
    return jnp.where(flag, x, 0.0), jnp.where(flag, 0.0, x)


def add(total, x):
    return total if x is None else x if total is None else total + x


STRIP = 64


def at(refs, layout, a, n):
    group, index = layout.spots[n]
    return refs[group].at[a, index]


def cols(ref, row, n, head):
    return ref[pl.ds(row, n), head * D : (head + 1) * D]


def weigh_blocks(layout, heads, q_ref, mask, vt_ref, s_ref, w_refs, old):
    tops = [[None, None] if old is None else list(old[a]) for a in range(heads)]
    for a in range(heads):
        for n, (keys, key_row, query_row, first, masked) in enumerate(layout.blocks):
            s = dot(keys[pl.ds(key_row, HALF), :D], cols(q_ref, query_row, HALF, a), NT)
            if masked:
                s = jnp.where(mask, s, -1e30)
            s_ref[a, n] = s
            top = jnp.max(s, axis=0, keepdims=True)
            for half in range(2):
                if first is (half == 1):
                    continue
                t = top
                if first is not True and first is not False:
                    t = jnp.where(first if half == 0 else jnp.logical_not(first), top, -1e30)
                tops[a][half] = t if tops[a][half] is None else jnp.maximum(tops[a][half], t)
    acc = [[None, None] for _ in range(heads)]
    for a in range(heads):
        for n, (keys, key_row, query_row, first, masked) in enumerate(layout.blocks):
            if first is True:
                m = tops[a][0]
            elif first is False:
                m = tops[a][1]
            else:
                m = jnp.where(first, tops[a][0], tops[a][1])
            w_ref = at(w_refs, layout, a, n)
            for r in range(0, HALF, STRIP):
                x = s_ref[a, n, r : r + STRIP, :]
                w_ref[r : r + STRIP, :] = jnp.exp2((x - m) * EXP2_SCALE).astype(bf16)
            for half, x in enumerate(split(first, dot(vt_ref[n], w_ref[...], NN))):
                acc[a][half] = add(acc[a][half], x)
    return tops, acc


def load_vt(layout, vt_ref):
    @pl.when(pl.program_id(0) == 0)
    def _():
        for n, (keys, key_row, *_) in enumerate(layout.blocks):
            vt_ref[n, :D, :] = jnp.transpose(keys[pl.ds(key_row, HALF), D:], (1, 0))
            vt_ref[n, D:, :] = jnp.ones((SUMS, HALF), bf16)


def fwd_first_kernel(heads, h_ref, q0, q1, q2, q3, own, *refs):
    n_win = (len(refs) - 6) // 2
    windows, refs = refs[:n_win], refs[n_win:]
    w_refs = refs[3 : 4 + n_win]
    q_out, state_ref, top_ref = refs[:3]
    vt_ref, s_ref = refs[4 + n_win :]
    h = h_ref[0]
    layout = Layout(h, own, windows, True)
    load_vt(layout, vt_ref)
    for k, piece in enumerate((q0, q1, q2, q3)):
        q_out[k * PIECE : (k + 1) * PIECE, :] = piece[...]
    tops, acc = weigh_blocks(layout, heads, q_out, causal(h), vt_ref, s_ref, w_refs, None)
    for a in range(heads):
        for half in range(2):
            state_ref[a, half] = acc[a][half]
            top_ref[a, half] = jnp.broadcast_to(tops[a][half], (8, HALF))


def fwd_last_kernel(heads, n_win, h_ref, q_ref, own, *refs):
    windows, (state_in, top_in), refs = refs[:n_win], refs[n_win : n_win + 2], refs[n_win + 2 :]
    o0, o1, o2, factor_ref = refs[:4]
    w_refs = refs[4 : 4 + n_win]
    vt_ref, s_ref, o_ref = refs[4 + n_win :]
    h = h_ref[0]
    layout = Layout(h, own, windows, False)
    load_vt(layout, vt_ref)
    old = [[top_in[a, half, :1, :] for half in range(2)] for a in range(heads)]
    tops, acc = weigh_blocks(layout, heads, q_ref, None, vt_ref, s_ref, w_refs, old)
    for a in range(heads):
        for half, row in enumerate((layout.q_early, layout.q_late)):
            shrink = jnp.exp2((old[a][half] - tops[a][half]) * EXP2_SCALE)
            t = state_in[a, half] * shrink + acc[a][half]
            r = 1.0 / t[D : D + 1]
            o_ref[pl.ds(row, HALF), a * D : (a + 1) * D] = jnp.transpose(t[:D] * r, (1, 0)).astype(bf16)
            factor_ref[a, half, 0:8] = jnp.broadcast_to(r * shrink, (8, HALF))
            factor_ref[a, half, 8:16] = jnp.broadcast_to(r, (8, HALF))
    for row, ref in ((0, o0), (PIECE, o1), (HALF, o2)):
        ref[...] = o_ref[row : row + ref.shape[0], :]


def scaled_kernel_part(heads, layout, g_pieces, o_pieces, factor_ref, g_ref, o_ref, ga_refs):
    for row, g, o in zip((0, PIECE, HALF), g_pieces, o_pieces):
        g_ref[row : row + g.shape[0], :] = g[...]
        o_ref[row : row + o.shape[0], :] = o[...]
    for a in range(heads):
        for half, row in enumerate((layout.q_early, layout.q_late)):
            g = cols(g_ref, row, HALF, a).astype(f32)
            out = cols(o_ref, row, HALF, a).astype(f32)
            for i, ref in enumerate(ga_refs):
                factor = jnp.broadcast_to(factor_ref[a, half, 8 * i : 8 * i + 1], (D, HALF))
                scaled = g * jnp.transpose(factor, (1, 0))
                ref[pl.ds(row, HALF), 2 * a * D : (2 * a + 1) * D] = scaled.astype(bf16)
                ref[pl.ds(row, HALF), (2 * a + 1) * D : (2 * a + 2) * D] = (-scaled * out).astype(bf16)


PAY_SPEC = pl.BlockSpec((ROWS + HEADER, 2 * D), lambda j, h: (0, 0))


def piece_spec(heads):
    return pl.BlockSpec((PIECE, heads * D), lambda j, h: (0, j))


def pieces_spec(heads):
    return [piece_spec(heads)] * 2 + [pl.BlockSpec((HALF, heads * D), lambda j, h: (0, j))]


def rows_spec(heads):
    return pl.BlockSpec((ROWS, heads * D), lambda j, h: (0, j))


def w_spec(heads, n):
    return pl.BlockSpec((heads, n, HALF, HALF), lambda j, h: (j, 0, 0, 0))


def half_spec(heads, n):
    return pl.BlockSpec((heads, 2, n, HALF), lambda j, h: (j, 0, 0, 0))


def call(kernel, name, steps, ins, in_specs, outs, out_specs, scratch, flops, exps=0, token=None):
    tokens = () if token is None else (token,)
    n = len(tokens)

    def body(h_ref, *refs):
        kernel(h_ref, *refs[n:])

    ins = (ins[0], *tokens, *ins[1:])
    in_specs = [pl.BlockSpec(memory_space=pl.ANY)] * n + in_specs
    return pl.pallas_call(
        body,
        grid_spec=pltpu.PrefetchScalarGridSpec(
            num_scalar_prefetch=1, grid=(steps,), in_specs=in_specs, out_specs=out_specs,
            scratch_shapes=scratch),
        out_shape=outs,
        compiler_params=pltpu.CompilerParams(vmem_limit_bytes=VMEM_LIMIT),
        cost_estimate=pl.CostEstimate(flops=flops, bytes_accessed=2**16, transcendentals=0),
        name=name,
    )(*ins)


def shape(*dims, dtype=bf16):
    return jax.ShapeDtypeStruct(dims, dtype)


STEP_FIRST, STEP_LAST, STEP_A, STEP_C = 2, 4, 2, 2


def forward_first(h, q, own, windows, token=None):
    heads = q[0].shape[1] // D
    n = 3 + 2 * len(windows)
    e = STEP_FIRST
    return call(
        functools.partial(fwd_first_kernel, e), "forward_first", heads // e, (h, *q, own, *windows),
        [piece_spec(e)] * 4 + [PAY_SPEC] * (1 + len(windows)),
        [shape(ROWS, heads * D), shape(heads, 2, D + SUMS, HALF, dtype=f32),
         shape(heads, 2, 8, HALF, dtype=f32), shape(heads, 3, HALF, HALF)]
        + [shape(heads, 2, HALF, HALF)] * len(windows),
        [rows_spec(e), half_spec(e, D + SUMS), half_spec(e, 8), w_spec(e, 3)]
        + [w_spec(e, 2)] * len(windows),
        [pltpu.VMEM((n, D + SUMS, HALF), bf16), pltpu.VMEM((e, n, HALF, HALF), f32)],
        int(heads * n * 1 * HALF * HALF * D), heads * n * HALF * HALF, token)


def forward_last(h, q_rows, own, windows, state, top):
    heads = q_rows.shape[1] // D
    e = STEP_LAST
    n_win = len(windows)
    n = 2 * n_win
    return call(
        functools.partial(fwd_last_kernel, e, n_win), "forward_last", heads // e,
        (h, q_rows, own, *windows, state, top),
        [rows_spec(e)] + [PAY_SPEC] * (1 + n_win) + [half_spec(e, D + SUMS), half_spec(e, 8)],
        [shape(PIECE, heads * D)] * 2 + [shape(HALF, heads * D), shape(heads, 2, 16, HALF, dtype=f32)]
        + [shape(heads, 2, HALF, HALF)] * n_win,
        pieces_spec(e) + [half_spec(e, 16)] + [w_spec(e, 2)] * n_win,
        [pltpu.VMEM((n, D + SUMS, HALF), bf16), pltpu.VMEM((e, n, HALF, HALF), f32),
         pltpu.VMEM((ROWS, e * D), bf16)],
        int(heads * n * 1 * HALF * HALF * D), heads * n * HALF * HALF)


def bwd_kernel(heads, n_win, with_own, first, last, which, h_ref, q_ref, own, *refs):
    if first:
        g_pieces, o_pieces, factor_ref, refs = refs[:3], refs[3:6], refs[6], refs[7:]
    else:
        ga_refs, refs = refs[:1], refs[1:]
    windows, refs = refs[:n_win], refs[n_win:]
    n_terms = n_win + with_own
    w_refs, refs = refs[:n_terms], refs[n_terms:]
    if not first:
        d_in, refs = refs[0], refs[1:]
    if last:
        d_outs, refs = refs[:3], refs[3:]
    else:
        d_out, ga_out, refs = refs[0], refs[1], refs[2:]
    terms, refs = refs[:n_terms], refs[n_terms:]
    kt_ref, va_ref, acc_ref, ds_ref = refs[:4]
    h = h_ref[0]
    layout = Layout(h, own, windows, with_own)
    j = pl.program_id(0)
    if first:
        g_ref, o_ref, gb_ref = refs[4:]
        ga_refs = (ga_out, gb_ref)
        scaled_kernel_part(heads, layout, g_pieces, o_pieces, factor_ref, g_ref, o_ref, ga_refs)

    @pl.when(j == 0)
    def _():
        for n, (keys, key_row, *_) in enumerate(layout.blocks):
            kt_ref[n] = jnp.transpose(keys[pl.ds(key_row, HALF), :D], (1, 0))
            va_ref[n, :, :D] = keys[pl.ds(key_row, HALF), D:]
            va_ref[n, :, D:] = jnp.ones((HALF, D), bf16)
        acc_ref[...] = jnp.zeros_like(acc_ref)

    total = [[None, None] if first else [d_in[a, 0], d_in[a, 1]] for a in range(heads)]

    def grads(n, row, a, width):
        ga_ref = ga_refs[which[layout.spots[n][0]]]
        return ga_ref[pl.ds(row, HALF), 2 * a * D : (2 * a + width) * D]

    for n, (keys, key_row, query_row, early, masked) in enumerate(layout.blocks):
        for a in range(heads):
            dp = dot(va_ref[n], grads(n, query_row, a, 2), NT)
            ds_ref[a, n] = (at(w_refs, layout, a, n)[...].astype(f32) * dp).astype(bf16)
    for n, (keys, key_row, query_row, early, masked) in enumerate(layout.blocks):
        value_sum = key_sum = None
        for a in range(heads):
            value_sum = add(value_sum, dot(at(w_refs, layout, a, n)[...], grads(n, query_row, a, 1), NN))
            key_sum = add(key_sum, dot(ds_ref[a, n], cols(q_ref, query_row, HALF, a), NN))
            for half, x in enumerate(split(early, dot(kt_ref[n], ds_ref[a, n], NN))):
                total[a][half] = add(total[a][half], x)
        acc_ref[n, :, D:] += value_sum
        acc_ref[n, :, :D] += key_sum
    if last:
        d_ref = refs[4]
        for a in range(heads):
            for row, d in ((layout.q_early, total[a][0]), (layout.q_late, total[a][1])):
                d_ref[pl.ds(row, HALF), a * D : (a + 1) * D] = jnp.transpose(d * SCALE, (1, 0)).astype(bf16)
        for row, ref in zip((0, PIECE, HALF), d_outs):
            ref[...] = d_ref[row : row + ref.shape[0], :]
    else:
        for a in range(heads):
            for half in range(2):
                d_out[a, half] = total[a][half]

    @pl.when(j == pl.num_programs(0) - 1)
    def _():
        n = 0
        for term in terms:
            if with_own and n == 0:
                parts = [(layout.q_early, acc_ref[0] + acc_ref[1]), (layout.q_late, acc_ref[2])]
                n = 3
            else:
                flag = layout.blocks[n + 1][3]
                k_early = layout.blocks[n][1]
                x, y = acc_ref[n], acc_ref[n + 1]
                parts = [
                    (k_early, x + jnp.where(flag, y, 0.0)),
                    (pl.multiple_of(HALF - k_early, HALF), jnp.where(flag, 0.0, y)),
                ]
                n += 2
            for row, x in parts:
                term[pl.ds(row, HALF), :D] = (x[:, :D] * SCALE).astype(bf16)
                term[pl.ds(row, HALF), D:] = x[:, D:].astype(bf16)


def backward(name, e, h, q_rows, cotangents, which, own, windows, w, d=None, with_own=False):
    heads = q_rows.shape[1] // D
    n = 3 * with_own + 2 * len(windows)
    n_terms = with_own + len(windows)
    first = d is None
    if first:
        specs = pieces_spec(e) * 2 + [half_spec(e, 16)]
        outs = [shape(heads, 2, D, HALF, dtype=f32), shape(ROWS, heads * 2 * D)]
        out_specs = [half_spec(e, D), rows_spec(2 * e)]
        scratch = [pltpu.VMEM((ROWS, e * D), bf16)] * 2 + [pltpu.VMEM((ROWS, 2 * e * D), bf16)]
    else:
        specs = [rows_spec(2 * e)]
        outs = [shape(PIECE, heads * D)] * 2 + [shape(HALF, heads * D)]
        out_specs = pieces_spec(e)
        scratch = [pltpu.VMEM((ROWS, e * D), bf16)]
    return call(
        functools.partial(bwd_kernel, e, len(windows), with_own, first, not first, which),
        name, heads // e,
        (h, q_rows, own, *cotangents, *windows, *w) + (() if first else (d,)),
        [rows_spec(e), PAY_SPEC] + specs + [PAY_SPEC] * len(windows)
        + [w_spec(e, 3)] * with_own + [w_spec(e, 2)] * len(windows)
        + ([] if first else [half_spec(e, D)]),
        outs + [shape(ROWS, 2 * D)] * n_terms,
        out_specs + [pl.BlockSpec((ROWS, 2 * D), lambda j, h: (0, 0))] * n_terms,
        [pltpu.VMEM((n, D, HALF), bf16), pltpu.VMEM((n, HALF, 2 * D), bf16),
         pltpu.VMEM((n, HALF, 2 * D), f32), pltpu.VMEM((e, n, HALF, HALF), bf16)] + scratch,
        int(heads * n * 2 * HALF * HALF * D))


def place_kernel(n, h_ref, *refs):
    pieces, outs, held, sems = refs[: 4 * n], refs[4 * n : 5 * n], refs[5 * n : -1], refs[-1]
    copies = []
    for i, out in enumerate(outs):
        width = pieces[4 * i].shape[1]
        for k in range(4):
            piece = pieces[4 * i + k]
            if out.dtype != bf16:
                held[0][k] = piece[...].astype(out.dtype)
                piece = held[0].at[k]
            column = pl.multiple_of((h_ref[0] ^ k) * width, width)
            copy = pltpu.make_async_copy(piece, out.at[:, pl.ds(column, width)], sems.at[4 * i + k])
            copy.start()
            copies.append(copy)
    for copy in copies:
        copy.wait()


def placed(h, *arrays):
    ins, outs, held = [], [], []
    for pieces, dtype in arrays:
        rows, width = pieces[0].shape
        ins += pieces
        outs.append(shape(rows, 4 * width, dtype=dtype))
        if dtype != bf16:
            held = [pltpu.VMEM((4, rows, width), dtype)]
    return pl.pallas_call(
        functools.partial(place_kernel, len(arrays)),
        in_specs=[pl.BlockSpec(memory_space=pltpu.SMEM)]
        + [pl.BlockSpec(memory_space=pltpu.VMEM)] * len(ins),
        out_specs=[pl.BlockSpec(memory_space=pl.ANY)] * len(outs),
        out_shape=outs,
        scratch_shapes=held + [pltpu.SemaphoreType.DMA((len(ins),))],
        cost_estimate=pl.CostEstimate(flops=0, bytes_accessed=2**21, transcendentals=0),
        name="placed",
    )(h, *ins)


def small(*arrays):
    return sum(a[:16, :D] for a in arrays)


def token(x, stages, name):
    for _ in range(stages):
        x = swap(x + 1, 1, name)
    return x


def together(*arrays):
    return lax.optimization_barrier(arrays)


def swap(x, k, name):
    with jax.named_scope(f"{name}_{k}"):
        return lax.ppermute(x, "head", [(i, i ^ k) for i in range(4)])


def along(x, axis, distance, name):
    n = lax.axis_size(axis)
    with jax.named_scope(name):
        return lax.ppermute(x, axis, [(i, (i + distance) % n) for i in range(n)])


def columns(h, x, k):
    width = x.shape[1] // 4
    return lax.dynamic_slice(x, (0, (h ^ k) * width), (x.shape[0], width))


def to_heads(h, x, name):
    return from_heads([columns(h, x, k) for k in range(4)], name)


def to_heads_by_two(h, x, name, earlier=()):
    near = swap(jnp.concatenate([columns(h, x, 1), columns(h, x, 3)], axis=0), 1, name)
    far = jnp.concatenate([columns(h, x, 2), near[PIECE:]], axis=0)
    if earlier:
        far, *earlier = together(far, *earlier)
    return [columns(h, x, 0), near, swap(far, 2, name)], earlier


def from_heads_by_two(pieces, name):
    own, partner, others = pieces
    far = swap(others, 2, name)
    return [own, swap(partner, 1, name), far[:PIECE], swap(far[PIECE:], 1, name)]


def from_heads(pieces, name):
    return [pieces[0]] + [swap(pieces[k], k, name) for k in (1, 2, 3)]


def plus(x, y):
    return (x.astype(f32) + y.astype(f32)).astype(bf16)


def local(query, key_value, grad_out, positions):
    h = lax.axis_index("head")
    h_arg = jnp.full((1,), h, jnp.int32)
    block = positions[0] // HALF
    b = jnp.where(h < 2, block, BLOCKS - 1 - block)
    header = jnp.broadcast_to(b.astype(bf16), (HEADER, 2 * D))
    kv = to_heads(h, key_value, "kv")
    own = jnp.concatenate(kv + [header], axis=0)
    w1 = along(own, "inner", 1, "w_1")
    before = along(own, ("inner", "outer"), 1, "before")
    w2 = along(w1, "inner", 1, "w_2")
    q = to_heads(h, query, "query")
    g, (q[2], q[3]) = to_heads_by_two(h, grad_out, "grad_out", (q[2], q[3]))
    q_token = token(small(before), 2, "before_token")
    w3 = along(w2, "inner", 1, "w_3")
    q_rows, state, top, wo, wwb, ww1 = forward_first(h_arg, q, own, [before, w1], q_token)
    *out, factors, ww2, ww3 = forward_last(h_arg, q_rows, own, [w2, w3], state, top)
    d, ga, t3, t2, tb = backward(
        "backward_first", STEP_A, h_arg, q_rows, (*g, *out, factors), (1, 1, 0), own,
        [w3, w2, before], [ww3, ww2, wwb])
    out = from_heads_by_two(out, "out")
    s2 = along(t3, "inner", -1, "term_3")
    back = along(tb, ("inner", "outer"), -1, "term_before")
    *dq, t0, t1 = backward(
        "backward_last", STEP_C, h_arg, q_rows, (ga,), (0, 0), own, [w1], [wo, ww1], d, with_own=True)
    s2, t1 = together(s2, t1)
    s1 = along(plus(t2, s2), "inner", -1, "term_2")
    s0 = along(plus(t1, s1), "inner", -1, "term_1")
    (attn_out,) = placed(h_arg, (out, bf16))
    dkv = (t0.astype(f32) + s0.astype(f32) + back.astype(f32)).astype(bf16)
    far = swap(dq[2], 2, "grad_query")
    far, attn_out = together(far, attn_out)
    dq = [dq[0], swap(dq[1], 1, "grad_query"), far[:PIECE], swap(far[PIECE:], 1, "grad_query")]
    dkv = from_heads([dkv[k * PIECE : (k + 1) * PIECE] for k in range(4)], "grad_kv")
    grad_query, grad_kv = placed(h_arg, (dq, bf16), (dkv, f32))
    return attn_out, grad_query, grad_kv


def solution(mesh):
    spec = P(("head", "inner", "outer"), None)
    return jax.shard_map(
        local,
        mesh=mesh,
        in_specs=(spec, spec, spec, P(("head", "inner", "outer"))),
        out_specs=(spec, spec, spec),
        check_vma=False,
    )
```

```python
import functools
import math

import jax
import jax.numpy as jnp
from jax import lax
from jax.experimental import pallas as pl
from jax.experimental.pallas import tpu as pltpu
from jax.sharding import PartitionSpec as P

D = 128
PIECE = 128
HALF = 256
ROWS = 512
HEADER = 16
BLOCKS = 128
SCALE = 1.0 / math.sqrt(D)
EXP2_SCALE = SCALE * math.log2(math.e)
VMEM_LIMIT = 26 * 2**20
f32, bf16 = jnp.float32, jnp.bfloat16
NT = (((1,), (1,)), ((), ()))
NN = (((1,), (0,)), ((), ()))
SUMS = 16


def dot(a, b, dims):
    return lax.dot_general(a, b, dims, preferred_element_type=f32)


def place(h, ref):
    b = jnp.max(ref[ROWS : ROWS + HEADER, :].astype(f32)).astype(jnp.int32)
    swapped = jnp.where(b < BLOCKS // 2, 0, 1) ^ (h // 2)
    early = pl.multiple_of(swapped * HALF, HALF)
    return jnp.minimum(b, BLOCKS - 1 - b), early, pl.multiple_of(HALF - early, HALF)


def causal(h):
    def position(axis):
        row = lax.broadcasted_iota(jnp.int32, (HALF, HALF), axis)
        return jnp.where(h % 2 == 0, row, (row + PIECE) % HALF)

    return position(0) <= position(1)


class Layout:
    def __init__(self, h, own_ref, windows, with_own):
        self.b, self.q_early, self.q_late = place(h, own_ref)
        self.blocks, self.spots = [], []
        if with_own:
            self.spots += [(0, 0), (0, 1), (0, 2)]
            self.blocks += [
                (own_ref, self.q_early, self.q_early, True, True),
                (own_ref, self.q_early, self.q_late, False, False),
                (own_ref, self.q_late, self.q_late, False, True),
            ]
        for group, ref in enumerate(windows):
            self.spots += [(group + with_own, 0), (group + with_own, 1)]
            b, k_early, k_late = place(h, ref)
            first = b < self.b
            key_row = pl.multiple_of(jnp.where(first, k_early, k_late), HALF)
            query_row = pl.multiple_of(jnp.where(first, self.q_early, self.q_late), HALF)
            self.blocks += [
                (ref, k_early, self.q_late, False, False),
                (ref, key_row, query_row, first, False),
            ]


def split(flag, x):
    if flag is True:
        return x, None
    if flag is False:
        return None, x
    return jnp.where(flag, x, 0.0), jnp.where(flag, 0.0, x)


def add(total, x):
    return total if x is None else x if total is None else total + x


STRIP = 64


def at(refs, layout, a, n):
    group, index = layout.spots[n]
    return refs[group].at[a, index]


def cols(ref, row, n, head):
    return ref[pl.ds(row, n), head * D : (head + 1) * D]


def weigh_blocks(layout, heads, q_ref, mask, vt_ref, s_ref, w_refs, old, piped):
    tops = [[None, None] if old is None else list(old[a]) for a in range(heads)]
    acc = [[None, None] for _ in range(heads)]

    def scores(a):
        for n, (keys, key_row, query_row, first, masked) in enumerate(layout.blocks):
            s = dot(keys[pl.ds(key_row, HALF), :D], cols(q_ref, query_row, HALF, a), NT)
            if masked:
                s = jnp.where(mask, s, -1e30)
            s_ref[a, n] = s
            top = jnp.max(s, axis=0, keepdims=True)
            for half in range(2):
                if first is (half == 1):
                    continue
                t = top
                if first is not True and first is not False:
                    t = jnp.where(first if half == 0 else jnp.logical_not(first), top, -1e30)
                tops[a][half] = t if tops[a][half] is None else jnp.maximum(tops[a][half], t)

    def sums(a):
        for n, (keys, key_row, query_row, first, masked) in enumerate(layout.blocks):
            if first is True:
                m = tops[a][0]
            elif first is False:
                m = tops[a][1]
            else:
                m = jnp.where(first, tops[a][0], tops[a][1])
            w_ref = at(w_refs, layout, a, n)
            for r in range(0, HALF, STRIP):
                x = s_ref[a, n, r : r + STRIP, :]
                w_ref[r : r + STRIP, :] = jnp.exp2((x - m) * EXP2_SCALE).astype(bf16)
            for half, x in enumerate(split(first, dot(vt_ref[n], w_ref[...], NN))):
                acc[a][half] = add(acc[a][half], x)

    for a in range(heads):
        scores(a)
        if piped and a:
            sums(a - 1)
    for a in range(heads - 1 if piped else 0, heads):
        sums(a)
    return tops, acc


def load_vt(layout, vt_ref):
    @pl.when(pl.program_id(0) == 0)
    def _():
        for n, (keys, key_row, *_) in enumerate(layout.blocks):
            vt_ref[n, :D, :] = jnp.transpose(keys[pl.ds(key_row, HALF), D:], (1, 0))
            vt_ref[n, D:, :] = jnp.ones((SUMS, HALF), bf16)


def fwd_first_kernel(heads, h_ref, q0, q1, q2, q3, own, *refs):
    n_win = (len(refs) - 6) // 2
    windows, refs = refs[:n_win], refs[n_win:]
    w_refs = refs[3 : 4 + n_win]
    q_out, state_ref, top_ref = refs[:3]
    vt_ref, s_ref = refs[4 + n_win :]
    h = h_ref[0]
    layout = Layout(h, own, windows, True)
    load_vt(layout, vt_ref)
    for k, piece in enumerate((q0, q1, q2, q3)):
        q_out[k * PIECE : (k + 1) * PIECE, :] = piece[...]
    tops, acc = weigh_blocks(layout, heads, q_out, causal(h), vt_ref, s_ref, w_refs, None, True)
    for a in range(heads):
        for half in range(2):
            state_ref[a, half] = acc[a][half]
            top_ref[a, half] = jnp.broadcast_to(tops[a][half], (8, HALF))


def fwd_last_kernel(heads, n_win, h_ref, q_ref, own, *refs):
    windows, (state_in, top_in), refs = refs[:n_win], refs[n_win : n_win + 2], refs[n_win + 2 :]
    o0, o1, o2, factor_ref = refs[:4]
    w_refs = refs[4 : 4 + n_win]
    vt_ref, s_ref, o_ref = refs[4 + n_win :]
    h = h_ref[0]
    layout = Layout(h, own, windows, False)
    load_vt(layout, vt_ref)
    old = [[top_in[a, half, :1, :] for half in range(2)] for a in range(heads)]
    tops, acc = weigh_blocks(layout, heads, q_ref, None, vt_ref, s_ref, w_refs, old, False)
    for a in range(heads):
        for half, row in enumerate((layout.q_early, layout.q_late)):
            shrink = jnp.exp2((old[a][half] - tops[a][half]) * EXP2_SCALE)
            t = state_in[a, half] * shrink + acc[a][half]
            r = 1.0 / t[D : D + 1]
            o_ref[pl.ds(row, HALF), a * D : (a + 1) * D] = jnp.transpose(t[:D] * r, (1, 0)).astype(bf16)
            factor_ref[a, half, 0:8] = jnp.broadcast_to(r * shrink, (8, HALF))
            factor_ref[a, half, 8:16] = jnp.broadcast_to(r, (8, HALF))
    for row, ref in ((0, o0), (PIECE, o1), (HALF, o2)):
        ref[...] = o_ref[row : row + ref.shape[0], :]


def scaled_kernel_part(heads, layout, g_pieces, o_pieces, factor_ref, g_ref, o_ref, ga_refs):
    for row, g, o in zip((0, PIECE, HALF), g_pieces, o_pieces):
        g_ref[row : row + g.shape[0], :] = g[...]
        o_ref[row : row + o.shape[0], :] = o[...]
    for a in range(heads):
        for half, row in enumerate((layout.q_early, layout.q_late)):
            g = cols(g_ref, row, HALF, a).astype(f32)
            out = cols(o_ref, row, HALF, a).astype(f32)
            for i, ref in enumerate(ga_refs):
                factor = jnp.broadcast_to(factor_ref[a, half, 8 * i : 8 * i + 1], (D, HALF))
                scaled = g * jnp.transpose(factor, (1, 0))
                ref[pl.ds(row, HALF), 2 * a * D : (2 * a + 1) * D] = scaled.astype(bf16)
                ref[pl.ds(row, HALF), (2 * a + 1) * D : (2 * a + 2) * D] = (-scaled * out).astype(bf16)


PAY_SPEC = pl.BlockSpec((ROWS + HEADER, 2 * D), lambda j, h: (0, 0))


def piece_spec(heads):
    return pl.BlockSpec((PIECE, heads * D), lambda j, h: (0, j))


def pieces_spec(heads):
    return [piece_spec(heads)] * 2 + [pl.BlockSpec((HALF, heads * D), lambda j, h: (0, j))]


def rows_spec(heads):
    return pl.BlockSpec((ROWS, heads * D), lambda j, h: (0, j))


def w_spec(heads, n):
    return pl.BlockSpec((heads, n, HALF, HALF), lambda j, h: (j, 0, 0, 0))


def half_spec(heads, n):
    return pl.BlockSpec((heads, 2, n, HALF), lambda j, h: (j, 0, 0, 0))


def call(kernel, name, steps, ins, in_specs, outs, out_specs, scratch, flops, exps=0, token=None):
    tokens = () if token is None else (token,)
    n = len(tokens)

    def body(h_ref, *refs):
        kernel(h_ref, *refs[n:])

    ins = (ins[0], *tokens, *ins[1:])
    in_specs = [pl.BlockSpec(memory_space=pl.ANY)] * n + in_specs
    return pl.pallas_call(
        body,
        grid_spec=pltpu.PrefetchScalarGridSpec(
            num_scalar_prefetch=1, grid=(steps,), in_specs=in_specs, out_specs=out_specs,
            scratch_shapes=scratch),
        out_shape=outs,
        compiler_params=pltpu.CompilerParams(vmem_limit_bytes=VMEM_LIMIT),
        cost_estimate=pl.CostEstimate(flops=flops, bytes_accessed=2**16, transcendentals=0),
        name=name,
    )(*ins)


def shape(*dims, dtype=bf16):
    return jax.ShapeDtypeStruct(dims, dtype)


STEP_FIRST, STEP_LAST, STEP_A, STEP_C = 4, 4, 4, 4


def forward_first(h, q, own, windows, token=None):
    heads = q[0].shape[1] // D
    n = 3 + 2 * len(windows)
    e = STEP_FIRST
    return call(
        functools.partial(fwd_first_kernel, e), "forward_first", heads // e, (h, *q, own, *windows),
        [piece_spec(e)] * 4 + [PAY_SPEC] * (1 + len(windows)),
        [shape(ROWS, heads * D), shape(heads, 2, D + SUMS, HALF, dtype=f32),
         shape(heads, 2, 8, HALF, dtype=f32), shape(heads, 3, HALF, HALF)]
        + [shape(heads, 2, HALF, HALF)] * len(windows),
        [rows_spec(e), half_spec(e, D + SUMS), half_spec(e, 8), w_spec(e, 3)]
        + [w_spec(e, 2)] * len(windows),
        [pltpu.VMEM((n, D + SUMS, HALF), bf16), pltpu.VMEM((e, n, HALF, HALF), f32)],
        int(heads * n * 1 * HALF * HALF * D), heads * n * HALF * HALF, token)


def forward_last(h, q_rows, own, windows, state, top):
    heads = q_rows.shape[1] // D
    e = STEP_LAST
    n_win = len(windows)
    n = 2 * n_win
    return call(
        functools.partial(fwd_last_kernel, e, n_win), "forward_last", heads // e,
        (h, q_rows, own, *windows, state, top),
        [rows_spec(e)] + [PAY_SPEC] * (1 + n_win) + [half_spec(e, D + SUMS), half_spec(e, 8)],
        [shape(PIECE, heads * D)] * 2 + [shape(HALF, heads * D), shape(heads, 2, 16, HALF, dtype=f32)]
        + [shape(heads, 2, HALF, HALF)] * n_win,
        pieces_spec(e) + [half_spec(e, 16)] + [w_spec(e, 2)] * n_win,
        [pltpu.VMEM((n, D + SUMS, HALF), bf16), pltpu.VMEM((e, n, HALF, HALF), f32),
         pltpu.VMEM((ROWS, e * D), bf16)],
        int(heads * n * 1 * HALF * HALF * D), heads * n * HALF * HALF)


def bwd_kernel(heads, n_win, with_own, first, last, which, h_ref, q_ref, own, *refs):
    if first:
        g_pieces, o_pieces, factor_ref, refs = refs[:3], refs[3:6], refs[6], refs[7:]
    else:
        ga_refs, refs = refs[:1], refs[1:]
    windows, refs = refs[:n_win], refs[n_win:]
    n_terms = n_win + with_own
    w_refs, refs = refs[:n_terms], refs[n_terms:]
    if not first:
        d_in, refs = refs[0], refs[1:]
    if last:
        d_outs, refs = refs[:3], refs[3:]
    else:
        d_out, ga_out, refs = refs[0], refs[1], refs[2:]
    terms, refs = refs[:n_terms], refs[n_terms:]
    kt_ref, va_ref, acc_ref, ds_ref = refs[:4]
    h = h_ref[0]
    layout = Layout(h, own, windows, with_own)
    j = pl.program_id(0)
    if first:
        g_ref, o_ref, gb_ref = refs[4:]
        ga_refs = (ga_out, gb_ref)
        scaled_kernel_part(heads, layout, g_pieces, o_pieces, factor_ref, g_ref, o_ref, ga_refs)

    @pl.when(j == 0)
    def _():
        for n, (keys, key_row, *_) in enumerate(layout.blocks):
            kt_ref[n] = jnp.transpose(keys[pl.ds(key_row, HALF), :D], (1, 0))
            va_ref[n, :, :D] = keys[pl.ds(key_row, HALF), D:]
            va_ref[n, :, D:] = jnp.ones((HALF, D), bf16)
        acc_ref[...] = jnp.zeros_like(acc_ref)

    total = [[None, None] if first else [d_in[a, 0], d_in[a, 1]] for a in range(heads)]

    def grads(n, row, a, width):
        ga_ref = ga_refs[which[layout.spots[n][0]]]
        return ga_ref[pl.ds(row, HALF), 2 * a * D : (2 * a + width) * D]

    for n, (keys, key_row, query_row, early, masked) in enumerate(layout.blocks):
        for a in range(heads):
            dp = dot(va_ref[n], grads(n, query_row, a, 2), NT)
            ds_ref[a, n] = (at(w_refs, layout, a, n)[...].astype(f32) * dp).astype(bf16)
    for n, (keys, key_row, query_row, early, masked) in enumerate(layout.blocks):
        value_sum = key_sum = None
        for a in range(heads):
            value_sum = add(value_sum, dot(at(w_refs, layout, a, n)[...], grads(n, query_row, a, 1), NN))
            key_sum = add(key_sum, dot(ds_ref[a, n], cols(q_ref, query_row, HALF, a), NN))
            for half, x in enumerate(split(early, dot(kt_ref[n], ds_ref[a, n], NN))):
                total[a][half] = add(total[a][half], x)
        acc_ref[n, :, D:] += value_sum
        acc_ref[n, :, :D] += key_sum
    if last:
        d_ref = refs[4]
        for a in range(heads):
            for row, d in ((layout.q_early, total[a][0]), (layout.q_late, total[a][1])):
                d_ref[pl.ds(row, HALF), a * D : (a + 1) * D] = jnp.transpose(d * SCALE, (1, 0)).astype(bf16)
        for row, ref in zip((0, PIECE, HALF), d_outs):
            ref[...] = d_ref[row : row + ref.shape[0], :]
    else:
        for a in range(heads):
            for half in range(2):
                d_out[a, half] = total[a][half]

    @pl.when(j == pl.num_programs(0) - 1)
    def _():
        n = 0
        for term in terms:
            if with_own and n == 0:
                parts = [(layout.q_early, acc_ref[0] + acc_ref[1]), (layout.q_late, acc_ref[2])]
                n = 3
            else:
                flag = layout.blocks[n + 1][3]
                k_early = layout.blocks[n][1]
                x, y = acc_ref[n], acc_ref[n + 1]
                parts = [
                    (k_early, x + jnp.where(flag, y, 0.0)),
                    (pl.multiple_of(HALF - k_early, HALF), jnp.where(flag, 0.0, y)),
                ]
                n += 2
            for row, x in parts:
                term[pl.ds(row, HALF), :D] = (x[:, :D] * SCALE).astype(bf16)
                term[pl.ds(row, HALF), D:] = x[:, D:].astype(bf16)


def backward(name, e, h, q_rows, cotangents, which, own, windows, w, d=None, with_own=False):
    heads = q_rows.shape[1] // D
    n = 3 * with_own + 2 * len(windows)
    n_terms = with_own + len(windows)
    first = d is None
    if first:
        specs = pieces_spec(e) * 2 + [half_spec(e, 16)]
        outs = [shape(heads, 2, D, HALF, dtype=f32), shape(ROWS, heads * 2 * D)]
        out_specs = [half_spec(e, D), rows_spec(2 * e)]
        scratch = [pltpu.VMEM((ROWS, e * D), bf16)] * 2 + [pltpu.VMEM((ROWS, 2 * e * D), bf16)]
    else:
        specs = [rows_spec(2 * e)]
        outs = [shape(PIECE, heads * D)] * 2 + [shape(HALF, heads * D)]
        out_specs = pieces_spec(e)
        scratch = [pltpu.VMEM((ROWS, e * D), bf16)]
    return call(
        functools.partial(bwd_kernel, e, len(windows), with_own, first, not first, which),
        name, heads // e,
        (h, q_rows, own, *cotangents, *windows, *w) + (() if first else (d,)),
        [rows_spec(e), PAY_SPEC] + specs + [PAY_SPEC] * len(windows)
        + [w_spec(e, 3)] * with_own + [w_spec(e, 2)] * len(windows)
        + ([] if first else [half_spec(e, D)]),
        outs + [shape(ROWS, 2 * D)] * n_terms,
        out_specs + [pl.BlockSpec((ROWS, 2 * D), lambda j, h: (0, 0))] * n_terms,
        [pltpu.VMEM((n, D, HALF), bf16), pltpu.VMEM((n, HALF, 2 * D), bf16),
         pltpu.VMEM((n, HALF, 2 * D), f32), pltpu.VMEM((e, n, HALF, HALF), bf16)] + scratch,
        int(heads * n * 2 * HALF * HALF * D))


def place_kernel(n, h_ref, *refs):
    pieces, outs, held, sems = refs[: 4 * n], refs[4 * n : 5 * n], refs[5 * n : -1], refs[-1]
    copies = []
    for i, out in enumerate(outs):
        width = pieces[4 * i].shape[1]
        for k in range(4):
            piece = pieces[4 * i + k]
            if out.dtype != bf16:
                held[0][k] = piece[...].astype(out.dtype)
                piece = held[0].at[k]
            column = pl.multiple_of((h_ref[0] ^ k) * width, width)
            copy = pltpu.make_async_copy(piece, out.at[:, pl.ds(column, width)], sems.at[4 * i + k])
            copy.start()
            copies.append(copy)
    for copy in copies:
        copy.wait()


def placed(h, *arrays):
    ins, outs, held = [], [], []
    for pieces, dtype in arrays:
        rows, width = pieces[0].shape
        ins += pieces
        outs.append(shape(rows, 4 * width, dtype=dtype))
        if dtype != bf16:
            held = [pltpu.VMEM((4, rows, width), dtype)]
    return pl.pallas_call(
        functools.partial(place_kernel, len(arrays)),
        in_specs=[pl.BlockSpec(memory_space=pltpu.SMEM)]
        + [pl.BlockSpec(memory_space=pltpu.VMEM)] * len(ins),
        out_specs=[pl.BlockSpec(memory_space=pl.ANY)] * len(outs),
        out_shape=outs,
        scratch_shapes=held + [pltpu.SemaphoreType.DMA((len(ins),))],
        cost_estimate=pl.CostEstimate(flops=0, bytes_accessed=2**21, transcendentals=0),
        name="placed",
    )(h, *ins)


def small(*arrays):
    return sum(a[:16, :D] for a in arrays)


def token(x, stages, name):
    for _ in range(stages):
        x = swap(x + 1, 1, name)
    return x


def together(*arrays):
    return lax.optimization_barrier(arrays)


def swap(x, k, name):
    with jax.named_scope(f"{name}_{k}"):
        return lax.ppermute(x, "head", [(i, i ^ k) for i in range(4)])


def along(x, axis, distance, name):
    n = lax.axis_size(axis)
    with jax.named_scope(name):
        return lax.ppermute(x, axis, [(i, (i + distance) % n) for i in range(n)])


def columns(h, x, k):
    width = x.shape[1] // 4
    return lax.dynamic_slice(x, (0, (h ^ k) * width), (x.shape[0], width))


def to_heads(h, x, name):
    return from_heads([columns(h, x, k) for k in range(4)], name)


def to_heads_by_two(h, x, name, earlier=()):
    near = swap(jnp.concatenate([columns(h, x, 1), columns(h, x, 3)], axis=0), 1, name)
    far = jnp.concatenate([columns(h, x, 2), near[PIECE:]], axis=0)
    if earlier:
        far, *earlier = together(far, *earlier)
    return [columns(h, x, 0), near, swap(far, 2, name)], earlier


def from_heads_by_two(pieces, name):
    own, partner, others = pieces
    far = swap(others, 2, name)
    return [own, swap(partner, 1, name), far[:PIECE], swap(far[PIECE:], 1, name)]


def from_heads(pieces, name):
    return [pieces[0]] + [swap(pieces[k], k, name) for k in (1, 2, 3)]


def plus(x, y):
    return (x.astype(f32) + y.astype(f32)).astype(bf16)


def local(query, key_value, grad_out, positions):
    h = lax.axis_index("head")
    h_arg = jnp.full((1,), h, jnp.int32)
    block = positions[0] // HALF
    b = jnp.where(h < 2, block, BLOCKS - 1 - block)
    header = jnp.broadcast_to(b.astype(bf16), (HEADER, 2 * D))
    kv = to_heads(h, key_value, "kv")
    own = jnp.concatenate(kv + [header], axis=0)
    w1 = along(own, "inner", 1, "w_1")
    before = along(own, ("inner", "outer"), 1, "before")
    w2 = along(w1, "inner", 1, "w_2")
    q = to_heads(h, query, "query")
    g, (q[2], q[3]) = to_heads_by_two(h, grad_out, "grad_out", (q[2], q[3]))
    q_token = token(small(before), 2, "before_token")
    w3 = along(w2, "inner", 1, "w_3")
    q_rows, state, top, wo, wwb, ww1 = forward_first(h_arg, q, own, [before, w1], q_token)
    *out, factors, ww2, ww3 = forward_last(h_arg, q_rows, own, [w2, w3], state, top)
    d, ga, t3, t2, tb = backward(
        "backward_first", STEP_A, h_arg, q_rows, (*g, *out, factors), (1, 1, 0), own,
        [w3, w2, before], [ww3, ww2, wwb])
    out = from_heads_by_two(out, "out")
    s2 = along(t3, "inner", -1, "term_3")
    back = along(tb, ("inner", "outer"), -1, "term_before")
    *dq, t0, t1 = backward(
        "backward_last", STEP_C, h_arg, q_rows, (ga,), (0, 0), own, [w1], [wo, ww1], d, with_own=True)
    s2, t1 = together(s2, t1)
    s1 = along(plus(t2, s2), "inner", -1, "term_2")
    s0 = along(plus(t1, s1), "inner", -1, "term_1")
    (attn_out,) = placed(h_arg, (out, bf16))
    dkv = (t0.astype(f32) + s0.astype(f32) + back.astype(f32)).astype(bf16)
    far = swap(dq[2], 2, "grad_query")
    far, attn_out = together(far, attn_out)
    dq = [dq[0], swap(dq[1], 1, "grad_query"), far[:PIECE], swap(far[PIECE:], 1, "grad_query")]
    dkv = from_heads([dkv[k * PIECE : (k + 1) * PIECE] for k in range(4)], "grad_kv")
    grad_query, grad_kv = placed(h_arg, (dq, bf16), (dkv, f32))
    return attn_out, grad_query, grad_kv


def solution(mesh):
    spec = P(("head", "inner", "outer"), None)
    return jax.shard_map(
        local,
        mesh=mesh,
        in_specs=(spec, spec, spec, P(("head", "inner", "outer"))),
        out_specs=(spec, spec, spec),
        check_vma=False,
    )
```

```python
import functools
import math

import jax
import jax.numpy as jnp
from jax import lax
from jax.experimental import pallas as pl
from jax.experimental.pallas import tpu as pltpu
from jax.sharding import PartitionSpec as P

D = 128
PIECE = 128
HALF = 256
ROWS = 512
HEADER = 16
BLOCKS = 128
SCALE = 1.0 / math.sqrt(D)
EXP2_SCALE = SCALE * math.log2(math.e)
VMEM_LIMIT = 26 * 2**20
f32, bf16 = jnp.float32, jnp.bfloat16
NT = (((1,), (1,)), ((), ()))
NN = (((1,), (0,)), ((), ()))
SUMS = 16


def dot(a, b, dims):
    return lax.dot_general(a, b, dims, preferred_element_type=f32)


def place(h, ref):
    b = jnp.max(ref[ROWS : ROWS + HEADER, :].astype(f32)).astype(jnp.int32)
    swapped = jnp.where(b < BLOCKS // 2, 0, 1) ^ (h // 2)
    early = pl.multiple_of(swapped * HALF, HALF)
    return jnp.minimum(b, BLOCKS - 1 - b), early, pl.multiple_of(HALF - early, HALF)


def causal(h):
    def position(axis):
        row = lax.broadcasted_iota(jnp.int32, (HALF, HALF), axis)
        return jnp.where(h % 2 == 0, row, (row + PIECE) % HALF)

    return position(0) <= position(1)


class Layout:
    def __init__(self, h, own_ref, windows, with_own):
        self.b, self.q_early, self.q_late = place(h, own_ref)
        self.blocks, self.spots = [], []
        if with_own:
            self.spots += [(0, 0), (0, 1), (0, 2)]
            self.blocks += [
                (own_ref, self.q_early, self.q_early, True, True),
                (own_ref, self.q_early, self.q_late, False, False),
                (own_ref, self.q_late, self.q_late, False, True),
            ]
        for group, ref in enumerate(windows):
            self.spots += [(group + with_own, 0), (group + with_own, 1)]
            b, k_early, k_late = place(h, ref)
            first = b < self.b
            key_row = pl.multiple_of(jnp.where(first, k_early, k_late), HALF)
            query_row = pl.multiple_of(jnp.where(first, self.q_early, self.q_late), HALF)
            self.blocks += [
                (ref, k_early, self.q_late, False, False),
                (ref, key_row, query_row, first, False),
            ]


def split(flag, x):
    if flag is True:
        return x, None
    if flag is False:
        return None, x
    return jnp.where(flag, x, 0.0), jnp.where(flag, 0.0, x)


def add(total, x):
    return total if x is None else x if total is None else total + x


STRIP = 64


def at(refs, layout, a, n):
    group, index = layout.spots[n]
    return refs[group].at[a, index]


def cols(ref, row, n, head):
    return ref[pl.ds(row, n), head * D : (head + 1) * D]


def weigh_blocks(layout, heads, q_ref, mask, vt_ref, s_ref, w_refs, old, piped):
    tops = [[None, None] if old is None else list(old[a]) for a in range(heads)]
    acc = [[None, None] for _ in range(heads)]

    def scores(a):
        for n, (keys, key_row, query_row, first, masked) in enumerate(layout.blocks):
            s = dot(keys[pl.ds(key_row, HALF), :D], cols(q_ref, query_row, HALF, a), NT)
            if masked:
                s = jnp.where(mask, s, -1e30)
            s_ref[a, n] = s
            top = jnp.max(s, axis=0, keepdims=True)
            for half in range(2):
                if first is (half == 1):
                    continue
                t = top
                if first is not True and first is not False:
                    t = jnp.where(first if half == 0 else jnp.logical_not(first), top, -1e30)
                tops[a][half] = t if tops[a][half] is None else jnp.maximum(tops[a][half], t)

    def sums(a):
        for n, (keys, key_row, query_row, first, masked) in enumerate(layout.blocks):
            if first is True:
                m = tops[a][0]
            elif first is False:
                m = tops[a][1]
            else:
                m = jnp.where(first, tops[a][0], tops[a][1])
            w_ref = at(w_refs, layout, a, n)
            for r in range(0, HALF, STRIP):
                x = s_ref[a, n, r : r + STRIP, :]
                w_ref[r : r + STRIP, :] = jnp.exp2((x - m) * EXP2_SCALE).astype(bf16)
            for half, x in enumerate(split(first, dot(vt_ref[n], w_ref[...], NN))):
                acc[a][half] = add(acc[a][half], x)

    for a in range(heads):
        scores(a)
        if piped and a:
            sums(a - 1)
    for a in range(heads - 1 if piped else 0, heads):
        sums(a)
    return tops, acc


def load_vt(layout, vt_ref):
    @pl.when(pl.program_id(0) == 0)
    def _():
        for n, (keys, key_row, *_) in enumerate(layout.blocks):
            vt_ref[n, :D, :] = jnp.transpose(keys[pl.ds(key_row, HALF), D:], (1, 0))
            vt_ref[n, D:, :] = jnp.ones((SUMS, HALF), bf16)


def fwd_first_kernel(heads, h_ref, q0, q1, q2, q3, own, *refs):
    n_win = (len(refs) - 6) // 2
    windows, refs = refs[:n_win], refs[n_win:]
    w_refs = refs[3 : 4 + n_win]
    q_out, state_ref, top_ref = refs[:3]
    vt_ref, s_ref = refs[4 + n_win :]
    h = h_ref[0]
    layout = Layout(h, own, windows, True)
    load_vt(layout, vt_ref)
    for k, piece in enumerate((q0, q1, q2, q3)):
        q_out[k * PIECE : (k + 1) * PIECE, :] = piece[...]
    tops, acc = weigh_blocks(layout, heads, q_out, causal(h), vt_ref, s_ref, w_refs, None, True)
    for a in range(heads):
        for half in range(2):
            state_ref[a, half] = acc[a][half]
            top_ref[a, half] = jnp.broadcast_to(tops[a][half], (8, HALF))


def fwd_last_kernel(heads, n_win, h_ref, q_ref, own, *refs):
    windows, (state_in, top_in), refs = refs[:n_win], refs[n_win : n_win + 2], refs[n_win + 2 :]
    o0, o1, o2, factor_ref = refs[:4]
    w_refs = refs[4 : 4 + n_win]
    vt_ref, s_ref, o_ref = refs[4 + n_win :]
    h = h_ref[0]
    layout = Layout(h, own, windows, False)
    load_vt(layout, vt_ref)
    old = [[top_in[a, half, :1, :] for half in range(2)] for a in range(heads)]
    tops, acc = weigh_blocks(layout, heads, q_ref, None, vt_ref, s_ref, w_refs, old, False)
    for a in range(heads):
        for half, row in enumerate((layout.q_early, layout.q_late)):
            shrink = jnp.exp2((old[a][half] - tops[a][half]) * EXP2_SCALE)
            t = state_in[a, half] * shrink + acc[a][half]
            r = 1.0 / t[D : D + 1]
            o_ref[pl.ds(row, HALF), a * D : (a + 1) * D] = jnp.transpose(t[:D] * r, (1, 0)).astype(bf16)
            factor_ref[a, half, 0:8] = jnp.broadcast_to(r * shrink, (8, HALF))
            factor_ref[a, half, 8:16] = jnp.broadcast_to(r, (8, HALF))
    for row, ref in ((0, o0), (PIECE, o1), (HALF, o2)):
        ref[...] = o_ref[row : row + ref.shape[0], :]


def scaled_kernel_part(heads, layout, g_pieces, o_pieces, factor_ref, g_ref, o_ref, ga_refs):
    for row, g, o in zip((0, PIECE, HALF), g_pieces, o_pieces):
        g_ref[row : row + g.shape[0], :] = g[...]
        o_ref[row : row + o.shape[0], :] = o[...]
    for a in range(heads):
        for half, row in enumerate((layout.q_early, layout.q_late)):
            g = cols(g_ref, row, HALF, a).astype(f32)
            out = cols(o_ref, row, HALF, a).astype(f32)
            for i, ref in enumerate(ga_refs):
                factor = jnp.broadcast_to(factor_ref[a, half, 8 * i : 8 * i + 1], (D, HALF))
                scaled = g * jnp.transpose(factor, (1, 0))
                ref[pl.ds(row, HALF), 2 * a * D : (2 * a + 1) * D] = scaled.astype(bf16)
                ref[pl.ds(row, HALF), (2 * a + 1) * D : (2 * a + 2) * D] = (-scaled * out).astype(bf16)


PAY_SPEC = pl.BlockSpec((ROWS + HEADER, 2 * D), lambda j, h: (0, 0))


def piece_spec(heads):
    return pl.BlockSpec((PIECE, heads * D), lambda j, h: (0, j))


def pieces_spec(heads):
    return [piece_spec(heads)] * 2 + [pl.BlockSpec((HALF, heads * D), lambda j, h: (0, j))]


def rows_spec(heads):
    return pl.BlockSpec((ROWS, heads * D), lambda j, h: (0, j))


def w_spec(heads, n):
    return pl.BlockSpec((heads, n, HALF, HALF), lambda j, h: (j, 0, 0, 0))


def half_spec(heads, n):
    return pl.BlockSpec((heads, 2, n, HALF), lambda j, h: (j, 0, 0, 0))


def call(kernel, name, steps, ins, in_specs, outs, out_specs, scratch, flops, exps=0, token=None):
    tokens = () if token is None else (token,)
    n = len(tokens)

    def body(h_ref, *refs):
        kernel(h_ref, *refs[n:])

    ins = (ins[0], *tokens, *ins[1:])
    in_specs = [pl.BlockSpec(memory_space=pl.ANY)] * n + in_specs
    return pl.pallas_call(
        body,
        grid_spec=pltpu.PrefetchScalarGridSpec(
            num_scalar_prefetch=1, grid=(steps,), in_specs=in_specs, out_specs=out_specs,
            scratch_shapes=scratch),
        out_shape=outs,
        compiler_params=pltpu.CompilerParams(vmem_limit_bytes=VMEM_LIMIT),
        cost_estimate=pl.CostEstimate(flops=flops, bytes_accessed=2**16, transcendentals=0),
        name=name,
    )(*ins)


def shape(*dims, dtype=bf16):
    return jax.ShapeDtypeStruct(dims, dtype)


STEP_FIRST, STEP_LAST, STEP_A, STEP_C = 4, 4, 4, 4


def forward_first(h, q, own, windows, token=None):
    heads = q[0].shape[1] // D
    n = 3 + 2 * len(windows)
    e = STEP_FIRST
    return call(
        functools.partial(fwd_first_kernel, e), "forward_first", heads // e, (h, *q, own, *windows),
        [piece_spec(e)] * 4 + [PAY_SPEC] * (1 + len(windows)),
        [shape(ROWS, heads * D), shape(heads, 2, D + SUMS, HALF, dtype=f32),
         shape(heads, 2, 8, HALF, dtype=f32), shape(heads, 3, HALF, HALF)]
        + [shape(heads, 2, HALF, HALF)] * len(windows),
        [rows_spec(e), half_spec(e, D + SUMS), half_spec(e, 8), w_spec(e, 3)]
        + [w_spec(e, 2)] * len(windows),
        [pltpu.VMEM((n, D + SUMS, HALF), bf16), pltpu.VMEM((e, n, HALF, HALF), f32)],
        int(heads * n * 1 * HALF * HALF * D), heads * n * HALF * HALF, token)


def forward_last(h, q_rows, own, windows, state, top):
    heads = q_rows.shape[1] // D
    e = STEP_LAST
    n_win = len(windows)
    n = 2 * n_win
    return call(
        functools.partial(fwd_last_kernel, e, n_win), "forward_last", heads // e,
        (h, q_rows, own, *windows, state, top),
        [rows_spec(e)] + [PAY_SPEC] * (1 + n_win) + [half_spec(e, D + SUMS), half_spec(e, 8)],
        [shape(PIECE, heads * D)] * 2 + [shape(HALF, heads * D), shape(heads, 2, 16, HALF, dtype=f32)]
        + [shape(heads, 2, HALF, HALF)] * n_win,
        pieces_spec(e) + [half_spec(e, 16)] + [w_spec(e, 2)] * n_win,
        [pltpu.VMEM((n, D + SUMS, HALF), bf16), pltpu.VMEM((e, n, HALF, HALF), f32),
         pltpu.VMEM((ROWS, e * D), bf16)],
        int(heads * n * 1 * HALF * HALF * D), heads * n * HALF * HALF)


def bwd_kernel(heads, n_win, with_own, first, last, which, h_ref, q_ref, own, *refs):
    if first:
        g_pieces, o_pieces, factor_ref, refs = refs[:3], refs[3:6], refs[6], refs[7:]
    else:
        ga_refs, refs = refs[:1], refs[1:]
    windows, refs = refs[:n_win], refs[n_win:]
    n_terms = n_win + with_own
    w_refs, refs = refs[:n_terms], refs[n_terms:]
    if not first:
        d_in, refs = refs[0], refs[1:]
    if last:
        d_outs, refs = refs[:3], refs[3:]
    else:
        d_out, ga_out, refs = refs[0], refs[1], refs[2:]
    terms, refs = refs[:n_terms], refs[n_terms:]
    kt_ref, va_ref, acc_ref, ds_ref = refs[:4]
    h = h_ref[0]
    layout = Layout(h, own, windows, with_own)
    j = pl.program_id(0)
    if first:
        g_ref, o_ref, gb_ref = refs[4:]
        ga_refs = (ga_out, gb_ref)
        scaled_kernel_part(heads, layout, g_pieces, o_pieces, factor_ref, g_ref, o_ref, ga_refs)

    @pl.when(j == 0)
    def _():
        for n, (keys, key_row, *_) in enumerate(layout.blocks):
            kt_ref[n] = jnp.transpose(keys[pl.ds(key_row, HALF), :D], (1, 0))
            va_ref[n, :, :D] = keys[pl.ds(key_row, HALF), D:]
            va_ref[n, :, D:] = jnp.ones((HALF, D), bf16)
        acc_ref[...] = jnp.zeros_like(acc_ref)

    total = [[None, None] if first else [d_in[a, 0], d_in[a, 1]] for a in range(heads)]

    def grads(n, row, a, width):
        ga_ref = ga_refs[which[layout.spots[n][0]]]
        return ga_ref[pl.ds(row, HALF), 2 * a * D : (2 * a + width) * D]

    for n, (keys, key_row, query_row, early, masked) in enumerate(layout.blocks):
        for a in range(heads):
            dp = dot(va_ref[n], grads(n, query_row, a, 2), NT)
            ds_ref[a, n] = (at(w_refs, layout, a, n)[...].astype(f32) * dp).astype(bf16)
    for n, (keys, key_row, query_row, early, masked) in enumerate(layout.blocks):
        value_sum = key_sum = None
        for a in range(heads):
            value_sum = add(value_sum, dot(at(w_refs, layout, a, n)[...], grads(n, query_row, a, 1), NN))
            key_sum = add(key_sum, dot(ds_ref[a, n], cols(q_ref, query_row, HALF, a), NN))
            for half, x in enumerate(split(early, dot(kt_ref[n], ds_ref[a, n], NN))):
                total[a][half] = add(total[a][half], x)
        acc_ref[n, :, D:] += value_sum
        acc_ref[n, :, :D] += key_sum
    if last:
        d_ref = refs[4]
        for a in range(heads):
            for row, d in ((layout.q_early, total[a][0]), (layout.q_late, total[a][1])):
                d_ref[pl.ds(row, HALF), a * D : (a + 1) * D] = jnp.transpose(d * SCALE, (1, 0)).astype(bf16)
        for row, ref in zip((0, PIECE, HALF), d_outs):
            ref[...] = d_ref[row : row + ref.shape[0], :]
    else:
        for a in range(heads):
            for half in range(2):
                d_out[a, half] = total[a][half]

    @pl.when(j == pl.num_programs(0) - 1)
    def _():
        n = 0
        for term in terms:
            if with_own and n == 0:
                parts = [(layout.q_early, acc_ref[0] + acc_ref[1]), (layout.q_late, acc_ref[2])]
                n = 3
            else:
                flag = layout.blocks[n + 1][3]
                k_early = layout.blocks[n][1]
                x, y = acc_ref[n], acc_ref[n + 1]
                parts = [
                    (k_early, x + jnp.where(flag, y, 0.0)),
                    (pl.multiple_of(HALF - k_early, HALF), jnp.where(flag, 0.0, y)),
                ]
                n += 2
            for row, x in parts:
                term[pl.ds(row, HALF), :D] = (x[:, :D] * SCALE).astype(bf16)
                term[pl.ds(row, HALF), D:] = x[:, D:].astype(bf16)


def backward(name, e, h, q_rows, cotangents, which, own, windows, w, d=None, with_own=False):
    heads = q_rows.shape[1] // D
    n = 3 * with_own + 2 * len(windows)
    n_terms = with_own + len(windows)
    first = d is None
    if first:
        specs = pieces_spec(e) * 2 + [half_spec(e, 16)]
        outs = [shape(heads, 2, D, HALF, dtype=f32), shape(ROWS, heads * 2 * D)]
        out_specs = [half_spec(e, D), rows_spec(2 * e)]
        scratch = [pltpu.VMEM((ROWS, e * D), bf16)] * 2 + [pltpu.VMEM((ROWS, 2 * e * D), bf16)]
    else:
        specs = [rows_spec(2 * e)]
        outs = [shape(PIECE, heads * D)] * 2 + [shape(HALF, heads * D)]
        out_specs = pieces_spec(e)
        scratch = [pltpu.VMEM((ROWS, e * D), bf16)]
    return call(
        functools.partial(bwd_kernel, e, len(windows), with_own, first, not first, which),
        name, heads // e,
        (h, q_rows, own, *cotangents, *windows, *w) + (() if first else (d,)),
        [rows_spec(e), PAY_SPEC] + specs + [PAY_SPEC] * len(windows)
        + [w_spec(e, 3)] * with_own + [w_spec(e, 2)] * len(windows)
        + ([] if first else [half_spec(e, D)]),
        outs + [shape(ROWS, 2 * D)] * n_terms,
        out_specs + [pl.BlockSpec((ROWS, 2 * D), lambda j, h: (0, 0))] * n_terms,
        [pltpu.VMEM((n, D, HALF), bf16), pltpu.VMEM((n, HALF, 2 * D), bf16),
         pltpu.VMEM((n, HALF, 2 * D), f32), pltpu.VMEM((e, n, HALF, HALF), bf16)] + scratch,
        int(heads * n * 2 * HALF * HALF * D))


PARTS = 4


def place_kernel(n, h_ref, *refs):
    pieces, outs, held, sems = refs[: 4 * n], refs[4 * n : 5 * n], refs[5 * n : -1], refs[-1]
    copies = []
    for i, out in enumerate(outs):
        width = pieces[4 * i].shape[1]
        for k in range(4):
            piece = pieces[4 * i + k]
            if out.dtype != bf16:
                held[0][k] = piece[...].astype(out.dtype)
                piece = held[0].at[k]
            column = pl.multiple_of((h_ref[0] ^ k) * width, width)
            for part in range(PARTS):
                rows = pl.ds(part * (PIECE // PARTS), PIECE // PARTS)
                copy = pltpu.make_async_copy(
                    piece.at[rows], out.at[rows, pl.ds(column, width)],
                    sems.at[(4 * i + k) * PARTS + part])
                copy.start()
                copies.append(copy)
    for copy in copies:
        copy.wait()


def placed(h, *arrays):
    ins, outs, held = [], [], []
    for pieces, dtype in arrays:
        rows, width = pieces[0].shape
        ins += pieces
        outs.append(shape(rows, 4 * width, dtype=dtype))
        if dtype != bf16:
            held = [pltpu.VMEM((4, rows, width), dtype)]
    return pl.pallas_call(
        functools.partial(place_kernel, len(arrays)),
        in_specs=[pl.BlockSpec(memory_space=pltpu.SMEM)]
        + [pl.BlockSpec(memory_space=pltpu.VMEM)] * len(ins),
        out_specs=[pl.BlockSpec(memory_space=pl.ANY)] * len(outs),
        out_shape=outs,
        scratch_shapes=held + [pltpu.SemaphoreType.DMA((len(ins) * PARTS,))],
        cost_estimate=pl.CostEstimate(flops=0, bytes_accessed=2**21, transcendentals=0),
        name="placed",
    )(h, *ins)


def small(*arrays):
    return sum(a[:16, :D] for a in arrays)


def token(x, stages, name):
    for _ in range(stages):
        x = swap(x + 1, 1, name)
    return x


def together(*arrays):
    return lax.optimization_barrier(arrays)


def swap(x, k, name):
    with jax.named_scope(f"{name}_{k}"):
        return lax.ppermute(x, "head", [(i, i ^ k) for i in range(4)])


def along(x, axis, distance, name):
    n = lax.axis_size(axis)
    with jax.named_scope(name):
        return lax.ppermute(x, axis, [(i, (i + distance) % n) for i in range(n)])


def columns(h, x, k):
    width = x.shape[1] // 4
    return lax.dynamic_slice(x, (0, (h ^ k) * width), (x.shape[0], width))


def to_heads(h, x, name):
    return from_heads([columns(h, x, k) for k in range(4)], name)


def to_heads_by_two(h, x, name, earlier=()):
    near = swap(jnp.concatenate([columns(h, x, 1), columns(h, x, 3)], axis=0), 1, name)
    far = jnp.concatenate([columns(h, x, 2), near[PIECE:]], axis=0)
    if earlier:
        far, *earlier = together(far, *earlier)
    return [columns(h, x, 0), near, swap(far, 2, name)], earlier


def from_heads_by_two(pieces, name):
    own, partner, others = pieces
    far = swap(others, 2, name)
    return [own, swap(partner, 1, name), far[:PIECE], swap(far[PIECE:], 1, name)]


def from_heads(pieces, name):
    return [pieces[0]] + [swap(pieces[k], k, name) for k in (1, 2, 3)]


def plus(x, y):
    return (x.astype(f32) + y.astype(f32)).astype(bf16)


def local(query, key_value, grad_out, positions):
    h = lax.axis_index("head")
    h_arg = jnp.full((1,), h, jnp.int32)
    block = positions[0] // HALF
    b = jnp.where(h < 2, block, BLOCKS - 1 - block)
    header = jnp.broadcast_to(b.astype(bf16), (HEADER, 2 * D))
    kv = to_heads(h, key_value, "kv")
    own = jnp.concatenate(kv + [header], axis=0)
    w1 = along(own, "inner", 1, "w_1")
    before = along(own, ("inner", "outer"), 1, "before")
    w2 = along(w1, "inner", 1, "w_2")
    q = to_heads(h, query, "query")
    g, (q[2], q[3]) = to_heads_by_two(h, grad_out, "grad_out", (q[2], q[3]))
    q_token = token(small(before), 2, "before_token")
    w3 = along(w2, "inner", 1, "w_3")
    q_rows, state, top, wo, wwb, ww1 = forward_first(h_arg, q, own, [before, w1], q_token)
    *out, factors, ww2, ww3 = forward_last(h_arg, q_rows, own, [w2, w3], state, top)
    d, ga, t3, t2, tb = backward(
        "backward_first", STEP_A, h_arg, q_rows, (*g, *out, factors), (1, 1, 0), own,
        [w3, w2, before], [ww3, ww2, wwb])
    out = from_heads_by_two(out, "out")
    s2 = along(t3, "inner", -1, "term_3")
    back = along(tb, ("inner", "outer"), -1, "term_before")
    *dq, t0, t1 = backward(
        "backward_last", STEP_C, h_arg, q_rows, (ga,), (0, 0), own, [w1], [wo, ww1], d, with_own=True)
    s2, t1 = together(s2, t1)
    s1 = along(plus(t2, s2), "inner", -1, "term_2")
    s0 = along(plus(t1, s1), "inner", -1, "term_1")
    (attn_out,) = placed(h_arg, (out, bf16))
    dkv = (t0.astype(f32) + s0.astype(f32) + back.astype(f32)).astype(bf16)
    far = swap(dq[2], 2, "grad_query")
    far, attn_out = together(far, attn_out)
    dq = [dq[0], swap(dq[1], 1, "grad_query"), far[:PIECE], swap(far[PIECE:], 1, "grad_query")]
    dkv = from_heads([dkv[k * PIECE : (k + 1) * PIECE] for k in range(4)], "grad_kv")
    grad_query, grad_kv = placed(h_arg, (dq, bf16), (dkv, f32))
    return attn_out, grad_query, grad_kv


def solution(mesh):
    spec = P(("head", "inner", "outer"), None)
    return jax.shard_map(
        local,
        mesh=mesh,
        in_specs=(spec, spec, spec, P(("head", "inner", "outer"))),
        out_specs=(spec, spec, spec),
        check_vma=False,
    )
```
